256 devices in a mesh: group: 16 (over x_hi, y, core), roll: 2 (over x_lo), tp: 8 (over z).
Axes of the slice: x: 4 (x_hi: 2, x_lo: 2; x = x_hi * 2 + x_lo), y: 4, z: 8, core: 2. Of those that a mesh axis runs over, the one named last changes fastest.
Arguments:
- vis_hidden: bfloat16 [4096, 5120], P('group'), may hold values from -6 to 6
- merge_weight: bfloat16 [5120, 8192], P('group', ('roll', 'tp')), may hold values from -0.078125 to 0.078125
- merge_bias: float32 [8192], P(('roll', 'tp')), may hold values from -3 to 3
- norm_gain: float32 [8192], replicated, may hold values from 0.1 to 1.9
- kv_weight: bfloat16 [8192, 2048], P(None, 'tp'), may hold values from -0.0625 to 0.0625
- kv_bias: float32 [2048], P('tp'), may hold values from -3 to 3
- queries: bfloat16 [32768, 8192], P(('group', 'roll'), 'tp'), may hold values from -26 to 26
- text_kv: bfloat16 [32768, 2048], P(('group', 'roll'), 'tp'), may hold values from -6 to 6
- image_count: int32 [16], P('group'), may hold values from 64 to 256, as said below
- image_pos: int32 [3, 4096], P(None, 'group'), may hold values from 0 to 4095
- resp_length: int32 [256], P(('group', 'roll')), may hold values from 32 to 128, as said below
Outputs:
- attended: bfloat16 [32768, 8192], P(('group', 'roll'), 'tp')
The draws below stay inside these ranges and needn't reach their ends.
Inputs may be any that keep to these rules, and one draw needn't show every extreme that they name: `image_count`: each prompt has at least a quarter of its 256 slots live, and some prompt has all 256 live. `resp_length`: each rollout has at least 32 tokens, and some rollout has all 128.
All inputs are finite; a program needn't handle non-finite values.
Results may differ from the reference program's by a relative error of at most 0.005.
Values may be sent and summed in bfloat16 or wider, within the bound.
A program may use at most 64 MiB of HBM per device.

```python
import jax
import jax.numpy as jnp
from jax import lax

D = 8192
VIS = 5120
HEADS = 64
KV_HEADS = 8
HEAD_DIM = 128
ROLLOUTS = 16
PIMG = 256
RLEN = 128
PROMPTS = 16
VIS_ROWS = 4096
TXT = 32768


def draw_queries(key, part):
    key = jax.random.fold_in(key, 7)
    drawn = jnp.clip(jax.random.normal(key, (TXT, KV_HEADS, HEADS // KV_HEADS, HEAD_DIM), jnp.float32), -6.0, 6.0)
    return drawn.reshape(TXT, HEADS * HEAD_DIM).astype(jnp.bfloat16)


def draw_text_kv(key, part):
    key = jax.random.fold_in(key, 5)
    drawn = jnp.clip(jax.random.normal(key, (TXT, KV_HEADS, 2, HEAD_DIM), jnp.float32), -6.0, 6.0)
    return drawn.reshape(TXT, KV_HEADS * 2 * HEAD_DIM).astype(jnp.bfloat16)


def draw_image_count(key, part):
    key = jax.random.fold_in(key, 3)
    counted = jax.random.randint(key, (PROMPTS,), PIMG // 4, PIMG + 1)
    filled = jax.random.randint(jax.random.fold_in(key, 1), (), 0, PROMPTS)
    return counted.at[filled].set(PIMG).astype(jnp.int32)


def draw_resp_length(key, part):
    key = jax.random.fold_in(key, 9)
    counted = jax.random.randint(key, (PROMPTS * ROLLOUTS,), RLEN // 4, RLEN + 1)
    filled = jax.random.randint(jax.random.fold_in(key, 1), (), 0, PROMPTS * ROLLOUTS)
    return counted.at[filled].set(RLEN).astype(jnp.int32)


def set_ends(values, rng, low, top_value):
    longest = values.shape.index(max(values.shape))
    spots = []
    for shift in (0, 1):
        where = [jax.random.randint(jax.random.fold_in(rng, axis), (), 0, length) for axis, length in enumerate(values.shape)]
        where[longest] = (where[longest] + shift) % values.shape[longest]
        spots.append(tuple(where))
    return values.at[spots[0]].set(low).at[spots[1]].set(top_value)


def level_of(rng, extent, pieces, low, high):
    def one(position, parts):
        steps = jax.random.uniform(jax.random.fold_in(jax.random.fold_in(rng, 6), position), (parts,), jnp.float32, low / len(pieces), high / len(pieces))
        return jnp.repeat(jnp.exp(steps), extent[position] // parts).reshape((-1,) + (1,) * (len(extent) - position - 1))

    factor_of = one(*pieces[0])
    for cut in pieces[1:]:
        factor_of = factor_of * one(*cut)
    return factor_of


def gaussian(stream_key, extent, scale, limit, pieces=(), kind=jnp.bfloat16):
    result = scale * jax.random.normal(stream_key, extent, jnp.float32)
    if pieces:
        result = result * level_of(stream_key, extent, pieces, -0.22, 0.18)
    return jnp.clip(result, -limit, limit).astype(kind)


def setup_inputs(seed: int = 0) -> dict:
    seeds = jax.random.split(jax.random.key(seed), 12)
    vis_hidden = gaussian(seeds[0], (VIS_ROWS, VIS), 1.0, 6.0, ((0, 16),))
    merge_weight = gaussian(seeds[1], (VIS, D), VIS ** -0.5, 0.078125, ((0, 16), (1, 16)))
    merge_bias = gaussian(seeds[2], (D,), 0.5, 3.0, ((0, 16),), jnp.float32)
    norm_gain = jnp.clip(1.0 + 0.18 * jax.random.normal(seeds[3], (D,), jnp.float32), 0.1, 1.9)
    kv_weight = gaussian(seeds[4], (D, KV_HEADS * 2 * HEAD_DIM), D ** -0.5, 0.0625, ((1, 8),))
    kv_bias = gaussian(seeds[5], (KV_HEADS * 2 * HEAD_DIM,), 0.5, 3.0, ((0, 8),), jnp.float32)
    queries = draw_queries(jax.random.fold_in(seeds[11], 71), 0)
    text_kv = draw_text_kv(jax.random.fold_in(seeds[11], 71), 0)
    image_count = draw_image_count(jax.random.fold_in(seeds[11], 71), 0)
    image_pos = set_ends(jax.random.randint(seeds[9], (3, VIS_ROWS), 0, 4096), jax.random.fold_in(seeds[9], 1), 0, 4095).astype(jnp.int32)
    resp_length = draw_resp_length(jax.random.fold_in(seeds[11], 71), 0)
    return {"vis_hidden": vis_hidden, "merge_weight": merge_weight, "merge_bias": merge_bias, "norm_gain": norm_gain, "kv_weight": kv_weight, "kv_bias": kv_bias, "queries": queries, "text_kv": text_kv, "image_count": image_count, "image_pos": image_pos, "resp_length": resp_length}


def rotate(key_part, positions):
    half_dim = key_part.shape[-1] // 2
    inverse = 1000000.0 ** (-jnp.arange(half_dim, dtype=jnp.float32) * 2.0 / key_part.shape[-1])
    freq_index = jnp.arange(half_dim)
    first_cut = half_dim // 4
    second_cut = first_cut + 3 * half_dim // 8
    pos_f = positions.astype(jnp.float32)
    chosen = jnp.where(freq_index[None, :] < first_cut, pos_f[0][:, None], jnp.where(freq_index[None, :] < second_cut, pos_f[1][:, None], pos_f[2][:, None]))
    angles = (chosen * inverse)[:, None, :]
    cosine = jnp.cos(angles)
    sine_part = jnp.sin(angles)
    first_half = key_part[..., :half_dim]
    second_half = key_part[..., half_dim:]
    return jnp.concatenate([first_half * cosine - second_half * sine_part, second_half * cosine + first_half * sine_part], axis=-1)

def reference(vis_hidden, merge_weight, merge_bias, norm_gain, kv_weight, kv_bias, queries, text_kv, image_count, image_pos, resp_length):
    per_group = HEADS // KV_HEADS
    factor = HEAD_DIM ** (-0.5)
    causal = jnp.arange(RLEN)[:, None] >= jnp.arange(RLEN)[None, :]

    def one_prompt(packed):
        hidden_rows, positions, live_count, query_rows, text_rows, lengths = packed
        activated = jax.nn.gelu(hidden_rows.astype(jnp.float32), approximate=False).astype(jnp.bfloat16)
        visual = (jnp.dot(activated, merge_weight, preferred_element_type=jnp.float32) + merge_bias).astype(jnp.bfloat16)
        values_f = visual.astype(jnp.float32)
        inv_rms = lax.rsqrt(lax.optimization_barrier(jnp.mean(values_f * values_f, axis=-1, keepdims=True)) + 1e-06)
        normed = (values_f * inv_rms * norm_gain).astype(jnp.bfloat16)
        projected = jnp.dot(normed, kv_weight, preferred_element_type=jnp.float32) + kv_bias
        projected = projected.reshape(PIMG, KV_HEADS, 2, HEAD_DIM)
        image_keys = rotate(projected[:, :, 0], positions).astype(jnp.bfloat16)
        image_values = projected[:, :, 1].astype(jnp.bfloat16)
        shaped_q = query_rows.reshape(ROLLOUTS, RLEN, KV_HEADS, per_group, HEAD_DIM).astype(jnp.float32)
        shaped_kv = text_rows.reshape(ROLLOUTS, RLEN, KV_HEADS, 2, HEAD_DIM).astype(jnp.float32)
        image_scores = jnp.einsum('rtkgd,jkd->rkgtj', shaped_q, image_keys.astype(jnp.float32)) * factor
        text_scores = jnp.einsum('rtkgd,rjkd->rkgtj', shaped_q, shaped_kv[:, :, :, 0]) * factor
        image_live = jnp.arange(PIMG) < live_count
        image_scores = jnp.where(image_live, image_scores, -1e+30)
        text_scores = jnp.where(causal, text_scores, -1e+30)
        highest = jnp.maximum(lax.optimization_barrier(jnp.max(image_scores, axis=-1)), lax.optimization_barrier(jnp.max(text_scores, axis=-1)))[..., None]
        image_exp = jnp.exp(image_scores - highest)
        text_exp = jnp.exp(text_scores - highest)
        denominator = lax.optimization_barrier(jnp.sum(image_exp, axis=-1, keepdims=True)) + lax.optimization_barrier(jnp.sum(text_exp, axis=-1, keepdims=True))
        image_weights = (image_exp / denominator).astype(jnp.bfloat16)
        text_weights = (text_exp / denominator).astype(jnp.bfloat16)
        context = jnp.einsum('rkgtj,jkd->rtkgd', image_weights.astype(jnp.float32), image_values.astype(jnp.float32))
        context = context + jnp.einsum('rkgtj,rjkd->rtkgd', text_weights.astype(jnp.float32), shaped_kv[:, :, :, 1])
        live_rows = jnp.arange(RLEN)[None, :] < lengths[:, None]
        context = jnp.where(live_rows[:, :, None, None, None], context, 0.0)
        return context.reshape(ROLLOUTS * RLEN, HEADS * HEAD_DIM).astype(jnp.bfloat16)
    stacked = lax.map(one_prompt, (vis_hidden.reshape(PROMPTS, PIMG, VIS), image_pos.reshape(3, PROMPTS, PIMG).transpose(1, 0, 2), image_count, queries.reshape(PROMPTS, ROLLOUTS * RLEN, HEADS * HEAD_DIM), text_kv.reshape(PROMPTS, ROLLOUTS * RLEN, KV_HEADS * 2 * HEAD_DIM), resp_length.reshape(PROMPTS, ROLLOUTS)))
    return stacked.reshape(TXT, HEADS * HEAD_DIM)
```

```python
import math

import jax
import jax.numpy as jnp
from jax import lax
from jax.experimental import pallas as pl
from jax.experimental.pallas import tpu as pltpu
from jax.sharding import PartitionSpec as P

HEAD_DIM = 128
RLEN = 128
MESH = pl.DeviceIdType.MESH
BF16 = jnp.bfloat16
F32 = jnp.float32

ZOFF = (0, 1, -1, 2, -2, 3, -3, 4)
ZBACK = (0, 2, 1, 4, 3, 6, 5, 7)
KVGROUPS = ((0, 3), (3, 2), (5, 3))
ROWS = 256
HALF = 128
HID = 320
PAIR = 640
COLS = 512


def gather_project_kernel(
    vis_hbm,
    w_hbm,
    kvw_hbm,
    mbias_ref,
    gain_ref,
    kvbias_ref,
    cos_ref,
    sin_ref,
    out_ref,
    vis,
    act,
    wbuf,
    kvbuf,
    acc,
    visual,
    xs,
    xg,
    sumsq,
    sumsq_in,
    sbuf,
    rbuf,
    res,
    res_in,
    local_sem,
    w_send,
    w_recv,
    kz_send,
    kz_recv,
    kx_send,
    kx_recv,
    v_sem,
    q_send,
    q_recv,
    p_send,
    p_recv,
    o_sem,
):
    g = lax.axis_index("group")
    roll = lax.axis_index("roll")
    z = lax.axis_index("tp")
    hi = g // 8
    y = lax.rem(g // 2, 4)
    core = lax.rem(g, 2)
    x = 2 * hi + roll
    me_k = hi * 4 + y

    def at(dx=0, dy=0, dz=0, sib=False):
        xx = lax.rem(x + dx + 4, 4)
        yy = lax.rem(y + dy + 4, 4)
        zz = lax.rem(z + dz + 8, 8)
        cc = 1 - core if sib else core
        return ((xx // 2) * 8 + yy * 2 + cc, lax.rem(xx, 2), zz)

    def k_of(dh, dy):
        hh = 1 - hi if dh else hi
        return hh * 4 + lax.rem(y + dy + 4, 4)

    started = []

    def send(src, dst, ssem, rsem, device):
        copy = pltpu.make_async_remote_copy(
            src_ref=src,
            dst_ref=dst,
            send_sem=ssem,
            recv_sem=rsem,
            device_id=device,
            device_id_type=MESH,
        )
        copy.start()
        started.append(copy)

    def arrived(dst, rsem):
        pltpu.make_async_remote_copy(
            src_ref=dst,
            dst_ref=dst,
            send_sem=rsem,
            recv_sem=rsem,
            device_id=at(sib=True),
            device_id_type=MESH,
        ).wait_recv()

    quarter = x * 2 + core
    kv_part = pl.ds(pl.multiple_of(quarter * HALF, HALF), HALF)

    def kv_rows(zz):
        start = (quarter // 4) * 4096 + zz * COLS + lax.rem(quarter, 4) * HALF
        return pl.ds(pl.multiple_of(start, HALF), HALF)

    own_w = pltpu.make_async_copy(
        w_hbm, wbuf.at[me_k, pl.ds(pl.multiple_of(core * HID, HID), HID)], local_sem.at[0]
    )
    own_kv = pltpu.make_async_copy(kvw_hbm.at[kv_rows(z)], kvbuf.at[0, kv_part], local_sem.at[1])
    own_vis = pltpu.make_async_copy(vis_hbm, vis, local_sem.at[2])
    own_w.start()
    own_kv.start()
    own_vis.start()

    partners = [at(dx=1), at(dx=-1), at(dx=2), at(dy=1), at(dy=-1), at(dy=2), at(sib=True)]
    partners += [at(dz=d) for d in ZOFF[1:]]
    barrier = pltpu.get_barrier_semaphore()
    for partner in partners:
        pl.semaphore_signal(barrier, inc=1, device_id=partner, device_id_type=MESH)
    pl.semaphore_wait(barrier, len(partners))

    def w_half(k, cc):
        return wbuf.at[k, pl.ds(pl.multiple_of(cc * HID, HID), HID)]

    slots = [(0, 0), (0, 1), (0, -1), (1, 0), (0, 2), (1, 1), (1, -1), (1, 2)]
    sent = iter(range(64))

    def w_forward(slot, targets):
        dh, dy = slots[slot]
        block = w_half(k_of(dh, dy), core)
        for dx, ddy in targets:
            there = ((dh + (1 if dx else 0)) % 2, (dy - ddy) % 4)
            index = [(a, b % 4) for a, b in slots].index(there)
            send(block, block, w_send.at[next(sent)], w_recv.at[index], at(dx=dx, dy=ddy))

    def w_sibling(slot):
        dh, dy = slots[slot]
        block = w_half(k_of(dh, dy), core)
        send(block, block, w_send.at[next(sent)], w_recv.at[8 + slot], at(sib=True))

    def w_wait(slot, from_sibling=False):
        dh, dy = slots[slot]
        cc = 1 - core if from_sibling else core
        arrived(w_half(k_of(dh, dy), cc), w_recv.at[8 * from_sibling + slot])

    own_w.wait()
    w_forward(0, [(2, 0)])
    for j in (7, 5, 6, 3, 4, 1, 2):
        zz = lax.rem(z + ZOFF[j] + 8, 8)
        send(
            kvw_hbm.at[kv_rows(zz)],
            kvbuf.at[ZBACK[j], kv_part],
            kz_send.at[j],
            kz_recv.at[ZBACK[j]],
            at(dz=ZOFF[j]),
        )
    w_forward(0, [(0, 1), (0, -1), (0, 2)])
    w_sibling(0)

    own_vis.wait()
    for k in range(8):
        v = vis[:, k * PAIR : (k + 1) * PAIR].astype(F32)
        act[k] = (v * (1.0 + lax.erf(v * (1.0 / math.sqrt(2.0)))) * 0.5).astype(BF16)

    def merge(slot, first=False):
        k = k_of(*slots[slot])
        part = jnp.dot(act[k], wbuf[k], preferred_element_type=F32)
        if first:
            acc[...] = part
        else:
            acc[...] += part

    kx_sent = iter(range(64))

    def kv_block(group, part):
        first, count = KVGROUPS[group]
        return kvbuf.at[pl.ds(first, count), pl.ds(pl.multiple_of(part * HALF, HALF), HALF)]

    def kv_share(group):
        first, count = KVGROUPS[group]
        for j in range(first, first + count):
            if j:
                arrived(kvbuf.at[j, kv_part], kz_recv.at[j])
        block = kv_block(group, quarter)
        for dx, source in ((2, 3), (1, 2), (-1, 1)):
            send(block, block, kx_send.at[next(kx_sent)], kx_recv.at[group * 7 + source], at(dx=dx))
        send(block, block, kx_send.at[next(kx_sent)], kx_recv.at[group * 7], at(sib=True))

    def part_at(dx, cc):
        return lax.rem(x + dx + 4, 4) * 2 + cc

    def kv_pass(group):
        for dx, source in ((1, 1), (-1, 2), (2, 3)):
            block = kv_block(group, part_at(dx, core))
            arrived(block, kx_recv.at[group * 7 + source])
            send(
                block,
                block,
                kx_send.at[next(kx_sent)],
                kx_recv.at[group * 7 + 3 + source],
                at(sib=True),
            )

    def kv_end(group):
        arrived(kv_block(group, part_at(0, 1 - core)), kx_recv.at[group * 7])
        for dx, source in ((1, 4), (-1, 5), (2, 6)):
            arrived(kv_block(group, part_at(dx, 1 - core)), kx_recv.at[group * 7 + source])

    own_kv.wait()
    w_wait(3)
    w_forward(3, [(0, 1), (0, -1), (0, 2)])
    w_sibling(3)
    kv_share(0)
    w_wait(0, True)
    merge(0, True)
    for slot in (1, 2):
        w_wait(slot)
        w_sibling(slot)
    kv_share(1)
    w_wait(3, True)
    merge(3)
    w_wait(4)
    w_sibling(4)
    kv_share(2)
    for slot in (1, 2, 4):
        w_wait(slot, True)
        merge(slot)
    kv_pass(0)
    for slot in (5, 6):
        w_wait(slot)
        w_sibling(slot)
    kv_pass(1)
    w_wait(7)
    w_sibling(7)
    kv_pass(2)
    for slot in (5, 6, 7):
        w_wait(slot, True)
        merge(slot)

    visual[...] = (acc[...] + mbias_ref[...]).astype(BF16)
    mine = pl.ds(pl.multiple_of(roll * HALF, HALF), HALF)
    theirs = pl.ds(pl.multiple_of((1 - roll) * HALF, HALF), HALF)
    partner = (g, 1 - roll, z)
    send(visual.at[theirs], xs.at[roll], v_sem.at[0], v_sem.at[1], partner)
    xs[roll] = visual[mine, :]
    for group in range(3):
        kv_end(group)
    arrived(xs.at[1 - roll], v_sem.at[1])

    total = jnp.zeros((HALF, 1), F32)
    for r in range(2):
        start = pl.multiple_of(r * 4096 + z * COLS, COLS)
        v = xs[r].astype(F32)
        total += jnp.sum(v * v, axis=1, keepdims=True)
        xg[r] = (v * gain_ref[:, pl.ds(start, COLS)]).astype(BF16)
    sumsq[...] = jnp.broadcast_to(total, (HALF, HALF)).T[:8]
    for j in range(1, 8):
        send(sumsq, sumsq_in.at[ZBACK[j]], q_send.at[j], q_recv.at[ZBACK[j]], at(dz=ZOFF[j]))

    def product(j):
        return jnp.dot(xg[0], kvbuf[j, :COLS], preferred_element_type=F32) + jnp.dot(
            xg[1], kvbuf[j, COLS:], preferred_element_type=F32
        )

    for j in (7, 5, 6, 3, 4, 1, 2):
        sbuf[j] = product(j).astype(BF16)
        send(sbuf.at[j], rbuf.at[ZBACK[j]], p_send.at[j], p_recv.at[ZBACK[j]], at(dz=ZOFF[j]))
    proj = product(0)
    square = sumsq[...]
    for j in range(1, 8):
        arrived(sumsq_in.at[j], q_recv.at[j])
        square += sumsq_in[j]
    inv = lax.rsqrt(square * (1.0 / 8192.0) + 1e-06)
    inv = jnp.broadcast_to(inv[:1], (HALF, HALF)).T
    for j in (1, 2, 3, 4, 5, 6, 7):
        arrived(rbuf.at[j], p_recv.at[j])
        proj += rbuf[j].astype(F32)
    key = proj[:, :HEAD_DIM] * inv + kvbias_ref[:, :HEAD_DIM]
    value = proj[:, HEAD_DIM:] * inv + kvbias_ref[:, HEAD_DIM:]
    key = key * cos_ref[mine, :] + pltpu.roll(key, HEAD_DIM // 2, 1) * sin_ref[mine, :]
    res[:, :HEAD_DIM] = key.astype(BF16)
    res[:, HEAD_DIM:] = value.astype(BF16)
    send(res, res_in, o_sem.at[0], o_sem.at[1], partner)
    out_ref[mine, :] = res[...]
    arrived(res_in, o_sem.at[1])
    out_ref[theirs, :] = res_in[...]
    for copy in started:
        copy.wait_send()


def gather_project(vis, w, kvw, mbias, gain, kvbias, cos, sin):
    vmem = pl.BlockSpec(memory_space=pltpu.VMEM)
    hbm = pl.BlockSpec(memory_space=pl.ANY)
    dma = pltpu.SemaphoreType.DMA
    return pl.pallas_call(
        gather_project_kernel,
        out_shape=jax.ShapeDtypeStruct((ROWS, 2 * HEAD_DIM), BF16),
        in_specs=[hbm, hbm, hbm, vmem, vmem, vmem, vmem, vmem],
        out_specs=vmem,
        scratch_shapes=[
            pltpu.VMEM((ROWS, 5120), BF16),
            pltpu.VMEM((8, ROWS, PAIR), BF16),
            pltpu.VMEM((8, PAIR, COLS), BF16),
            pltpu.VMEM((8, 1024, 2 * HEAD_DIM), BF16),
            pltpu.VMEM((ROWS, COLS), F32),
            pltpu.VMEM((ROWS, COLS), BF16),
            pltpu.VMEM((2, HALF, COLS), BF16),
            pltpu.VMEM((2, HALF, COLS), BF16),
            pltpu.VMEM((8, HALF), F32),
            pltpu.VMEM((8, 8, HALF), F32),
            pltpu.VMEM((8, HALF, 2 * HEAD_DIM), BF16),
            pltpu.VMEM((8, HALF, 2 * HEAD_DIM), BF16),
            pltpu.VMEM((HALF, 2 * HEAD_DIM), BF16),
            pltpu.VMEM((HALF, 2 * HEAD_DIM), BF16),
            dma((3,)),
            dma((16,)),
            dma((16,)),
            dma((8,)),
            dma((8,)),
            dma((24,)),
            dma((24,)),
            dma((2,)),
            dma((8,)),
            dma((8,)),
            dma((8,)),
            dma((8,)),
            dma((2,)),
        ],
        compiler_params=pltpu.CompilerParams(
            collective_id=0, has_side_effects=True, vmem_limit_bytes=44 * 2**20
        ),
        cost_estimate=pl.CostEstimate(
            flops=2_500_000_000, bytes_accessed=8_000_000, transcendentals=1_500_000
        ),
        name="gather_project",
    )(vis, w, kvw, mbias, gain, kvbias, cos, sin)


def attention_kernel(count_ref, length_ref, q_ref, tkv_ref, kv_ref, out_ref):
    step = pl.program_id(0)
    live_count = count_ref[0]
    length = length_ref[step]
    keys = jnp.concatenate([kv_ref[:, :HEAD_DIM], tkv_ref[:, :HEAD_DIM]], axis=0)
    values = jnp.concatenate([kv_ref[:, HEAD_DIM:], tkv_ref[:, HEAD_DIM:]], axis=0)
    width = ROWS + RLEN
    values = jnp.concatenate([values, jnp.ones((width, HEAD_DIM), BF16)], axis=1)
    row = lax.broadcasted_iota(jnp.int32, (RLEN, width), 0)
    col = lax.broadcasted_iota(jnp.int32, (RLEN, width), 1)
    live = col < jnp.where(col < ROWS, live_count, row + (ROWS + 1))
    kept = lax.broadcasted_iota(jnp.int32, (RLEN, HEAD_DIM), 0) < length
    factor = HEAD_DIM ** (-0.5) * math.log2(math.e)
    for h in range(8):
        cols = slice(h * HEAD_DIM, (h + 1) * HEAD_DIM)
        scores = lax.dot_general(
            q_ref[:, cols], keys, (((1,), (1,)), ((), ())), preferred_element_type=F32
        )
        scores = jnp.where(live, scores, -1e30)
        highest = jnp.max(scores, axis=1, keepdims=True)
        weights = jnp.exp2((scores - highest) * factor).astype(BF16)
        sums = jnp.dot(weights, values, preferred_element_type=F32)
        attended = sums[:, :HEAD_DIM] / sums[:, HEAD_DIM:]
        out_ref[:, cols] = jnp.where(kept, attended, 0.0).astype(BF16)


def attention(count, length, q, tkv, kv):
    rollouts = length.shape[0]
    return pl.pallas_call(
        attention_kernel,
        grid_spec=pltpu.PrefetchScalarGridSpec(
            num_scalar_prefetch=2,
            grid=(rollouts,),
            in_specs=[
                pl.BlockSpec((RLEN, q.shape[1]), lambda i, *_: (i, 0)),
                pl.BlockSpec((RLEN, tkv.shape[1]), lambda i, *_: (i, 0)),
                pl.BlockSpec(kv.shape, lambda i, *_: (0, 0)),
            ],
            out_specs=pl.BlockSpec((RLEN, q.shape[1]), lambda i, *_: (i, 0)),
        ),
        out_shape=jax.ShapeDtypeStruct(q.shape, BF16),
        compiler_params=pltpu.CompilerParams(vmem_limit_bytes=24 * 2**20),
        name="attention",
    )(count, length, q, tkv, kv)


def rotary_tables(positions):
    half_dim = HEAD_DIM // 2
    inverse = 1000000.0 ** (-jnp.arange(half_dim, dtype=F32) * 2.0 / HEAD_DIM)
    freq_index = jnp.arange(half_dim)
    first_cut = half_dim // 4
    second_cut = first_cut + 3 * half_dim // 8
    pos_f = positions.astype(F32)
    chosen = jnp.where(
        freq_index[None, :] < first_cut,
        pos_f[0][:, None],
        jnp.where(freq_index[None, :] < second_cut, pos_f[1][:, None], pos_f[2][:, None]),
    )
    angles = chosen * inverse
    cosine = jnp.cos(angles)
    sine = jnp.sin(angles)
    return jnp.concatenate([cosine, cosine], axis=1), jnp.concatenate([-sine, sine], axis=1)


def body(
    vis_hidden,
    merge_weight,
    merge_bias,
    norm_gain,
    kv_weight,
    kv_bias,
    queries,
    text_kv,
    image_count,
    image_pos,
    resp_length,
):
    cos, sin = rotary_tables(image_pos)
    kv = gather_project(
        vis_hidden,
        merge_weight,
        kv_weight,
        merge_bias.reshape(1, -1),
        norm_gain.reshape(1, -1),
        kv_bias.reshape(1, -1),
        cos,
        sin,
    )
    return attention(image_count, resp_length, queries, text_kv, kv)


def solution(mesh):
    in_specs = (
        P("group", None),
        P("group", ("roll", "tp")),
        P(("roll", "tp")),
        P(),
        P(None, "tp"),
        P("tp"),
        P(("group", "roll"), "tp"),
        P(("group", "roll"), "tp"),
        P("group"),
        P(None, "group"),
        P(("group", "roll")),
    )
    out_specs = P(("group", "roll"), "tp")
    return jax.shard_map(body, mesh=mesh, in_specs=in_specs, out_specs=out_specs, check_vma=False)
```

```python
import math

import jax
import jax.numpy as jnp
from jax import lax
from jax.experimental import pallas as pl
from jax.experimental.pallas import tpu as pltpu
from jax.sharding import PartitionSpec as P

HEAD_DIM = 128
RLEN = 128
BATCH = 8
UNROLL = 2
MESH = pl.DeviceIdType.MESH
BF16 = jnp.bfloat16
F32 = jnp.float32

ZOFF = (0, 1, -1, 2, -2, 3, -3, 4)
ZBACK = (0, 2, 1, 4, 3, 6, 5, 7)
KVGROUPS = ((0, 3), (3, 2), (5, 3))
SLOTS = [(0, 0), (0, 1), (0, -1), (1, 0), (0, 2), (1, 1), (1, -1), (1, 2)]
NEXT_UP, NEXT_DOWN, CROSS, FAR, CROSS_UP, CROSS_DOWN, CROSS_FAR = range(1, 8)
ROWS = 256
HALF = 128
HID = 320
PAIR = 640
COLS = 512


def gather_project_kernel(
    vis_hbm,
    w_hbm,
    kvw_hbm,
    mbias_hbm,
    gain_hbm,
    kvbias_hbm,
    pos_hbm,
    out_ref,
    mbias_ref,
    gain_ref,
    kvbias_ref,
    pos_ref,
    cos_ref,
    sin_ref,
    vis,
    act,
    wbuf,
    kvbuf,
    acc,
    visual,
    xs,
    xg,
    sumsq,
    sumsq_in,
    sbuf,
    rbuf,
    proj,
    res,
    res_in,
    local_sem,
    w_send,
    w_recv,
    kz_send,
    kz_recv,
    kx_send,
    kx_recv,
    v_sem,
    q_send,
    q_recv,
    p_send,
    p_recv,
    o_sem,
):
    g = lax.axis_index("group")
    roll = lax.axis_index("roll")
    z = lax.axis_index("tp")
    hi = g // 8
    y = lax.rem(g // 2, 4)
    core = lax.rem(g, 2)
    x = 2 * hi + roll
    me_k = hi * 4 + y

    def at(dx=0, dy=0, dz=0, sib=False):
        xx = lax.rem(x + dx + 4, 4)
        yy = lax.rem(y + dy + 4, 4)
        zz = lax.rem(z + dz + 8, 8)
        cc = 1 - core if sib else core
        return ((xx // 2) * 8 + yy * 2 + cc, lax.rem(xx, 2), zz)

    def k_of(dh, dy):
        hh = 1 - hi if dh else hi
        return hh * 4 + lax.rem(y + dy + 4, 4)

    started = []

    def send(src, dst, ssem, rsem, device):
        copy = pltpu.make_async_remote_copy(
            src_ref=src,
            dst_ref=dst,
            send_sem=ssem,
            recv_sem=rsem,
            device_id=device,
            device_id_type=MESH,
        )
        copy.start()
        started.append(copy)

    def arrived(dst, rsem):
        pltpu.make_async_remote_copy(
            src_ref=dst,
            dst_ref=dst,
            send_sem=rsem,
            recv_sem=rsem,
            device_id=at(sib=True),
            device_id_type=MESH,
        ).wait_recv()

    part_start = roll * COLS + core * ROWS

    def kv_piece(first, count, start, rows):
        return kvbuf.at[pl.ds(first, count), pl.ds(pl.multiple_of(start, HALF), rows)]

    def kv_rows(zz):
        start = roll * 4096 + zz * COLS + core * ROWS
        return pl.ds(pl.multiple_of(start, ROWS), ROWS)

    def kv_slot(j):
        return kvbuf.at[j, pl.ds(pl.multiple_of(part_start, ROWS), ROWS)]

    def w_piece(slot, half, cc):
        dh, dy = SLOTS[slot]
        start, rows = (0, HID) if half is None else (half * (HID // 2), HID // 2)
        return wbuf.at[k_of(dh, dy), pl.ds(pl.multiple_of(cc * HID + start, 32), rows)]

    own_w = pltpu.make_async_copy(w_hbm, w_piece(0, None, core), local_sem.at[0])
    own_kv = pltpu.make_async_copy(kvw_hbm.at[kv_rows(z)], kv_slot(0), local_sem.at[1])
    own_vis = pltpu.make_async_copy(vis_hbm, vis, local_sem.at[2])
    own_w.start()
    own_kv.start()
    own_vis.start()
    small = [
        pltpu.make_async_copy(src, dst, local_sem.at[3 + i])
        for i, (src, dst) in enumerate(
            (
                (mbias_hbm, mbias_ref),
                (gain_hbm, gain_ref),
                (kvbias_hbm, kvbias_ref),
                (pos_hbm, pos_ref),
            )
        )
    ]
    for copy in small:
        copy.start()

    partners = [at(dx=1), at(dx=-1), at(dx=2), at(dy=1), at(dy=-1), at(dy=2), at(sib=True)]
    partners += [at(dz=d) for d in ZOFF[1:]]
    barrier = pltpu.get_barrier_semaphore()
    for partner in partners:
        pl.semaphore_signal(barrier, inc=1, device_id=partner, device_id_type=MESH)
    pl.semaphore_wait(barrier, len(partners))

    sent = iter(range(64))
    kx_sent = iter(range(64))

    def w_send_to(slot, half, dx=0, dy=0):
        dh, ddy = SLOTS[slot]
        there = SLOTS.index(((dh + (1 if dx else 0)) % 2, (ddy - dy + 1) % 4 - 1))
        block = w_piece(slot, half, core)
        send(block, block, w_send.at[next(sent)], w_recv.at[there * 2 + half], at(dx=dx, dy=dy))

    def w_wait(slot, half):
        arrived(w_piece(slot, half, core), w_recv.at[slot * 2 + half])

    def w_sibling(slot, half=None):
        block = w_piece(slot, half, core)
        index = 16 + slot * 2 + (half or 0)
        send(block, block, w_send.at[next(sent)], w_recv.at[index], at(sib=True))

    def w_sibling_wait(slot, half=None):
        arrived(w_piece(slot, half, 1 - core), w_recv.at[16 + slot * 2 + (half or 0)])

    own_w.wait()
    for half in (0, 1):
        w_send_to(0, half, dx=2)
    for half in (0, 1):
        w_send_to(0, half, dy=1)
        w_send_to(0, 1 - half, dy=-1)
    for j in (1, 2, 3, 4, 5, 6, 7):
        zz = lax.rem(z + ZOFF[j] + 8, 8)
        send(
            kvw_hbm.at[kv_rows(zz)],
            kv_slot(ZBACK[j]),
            kz_send.at[j],
            kz_recv.at[ZBACK[j]],
            at(dz=ZOFF[j]),
        )
    w_sibling(0)

    own_vis.wait()

    def activate(k):
        def step(i, carry):
            rows = pl.ds(pl.multiple_of(i * 32, 32), 32)
            v = vis[rows, k * PAIR : (k + 1) * PAIR].astype(F32)
            act[k, rows] = (v * (1.0 + lax.erf(v * (1.0 / math.sqrt(2.0)))) * 0.5).astype(BF16)
            return carry

        lax.fori_loop(0, ROWS // 32, step, 0)

    def merge(count, chip):
        def step(i, carry):
            k = chip(i)
            acc[...] += jnp.dot(act[k], wbuf[k], preferred_element_type=F32)
            return carry

        lax.fori_loop(0, count, step, 0)

    def kv_share(group):
        first, count = KVGROUPS[group]
        for j in range(first, first + count):
            if j:
                arrived(kv_slot(j), kz_recv.at[j])
        for i, dx in ((0, 1), (1, -1)):
            block = kv_piece(first, count, part_start + i * HALF, HALF)
            send(block, block, kx_send.at[next(kx_sent)], kx_recv.at[group * 4 + i], at(dx=dx))
        block = kv_piece(first, count, part_start, ROWS)
        send(block, block, kx_send.at[next(kx_sent)], kx_recv.at[group * 4 + 2], at(sib=True))

    other_start = (1 - roll) * COLS + core * ROWS

    def kv_pass(group):
        first, count = KVGROUPS[group]
        for i in (0, 1):
            block = kv_piece(first, count, other_start + i * HALF, HALF)
            arrived(block, kx_recv.at[group * 4 + i])
        block = kv_piece(first, count, other_start, ROWS)
        send(block, block, kx_send.at[next(kx_sent)], kx_recv.at[group * 4 + 3], at(sib=True))

    def kv_end(group):
        first, count = KVGROUPS[group]
        for i, rr in ((2, roll), (3, 1 - roll)):
            block = kv_piece(first, count, rr * COLS + (1 - core) * ROWS, ROWS)
            arrived(block, kx_recv.at[group * 4 + i])

    activate(0)
    activate(1)
    w_wait(NEXT_DOWN, 0)
    w_send_to(NEXT_DOWN, 0, dy=1)
    w_wait(NEXT_UP, 1)
    w_send_to(NEXT_UP, 1, dy=-1)
    activate(2)
    for half in (0, 1):
        w_wait(CROSS, half)
        w_send_to(CROSS, half, dy=1)
        w_send_to(CROSS, half, dy=-1)
        activate(3 + half)
    own_kv.wait()
    kv_share(0)
    w_sibling(CROSS)
    w_wait(NEXT_DOWN, 1)
    w_sibling(NEXT_DOWN)
    w_wait(NEXT_UP, 0)
    w_sibling(NEXT_UP)
    activate(5)
    kv_share(1)
    w_wait(CROSS_DOWN, 0)
    w_send_to(CROSS_DOWN, 0, dy=1)
    w_wait(CROSS_UP, 1)
    w_send_to(CROSS_UP, 1, dy=-1)
    activate(6)
    for half in (0, 1):
        w_wait(FAR, half)
    w_sibling(FAR)
    kv_share(2)
    activate(7)
    for copy in small:
        copy.wait()
    mine = pl.ds(pl.multiple_of(roll * HALF, HALF), HALF)
    theirs = pl.ds(pl.multiple_of((1 - roll) * HALF, HALF), HALF)
    lane = lax.broadcasted_iota(jnp.int32, (HALF, HEAD_DIM), 1)
    freq = lax.rem(lane, HEAD_DIM // 2)
    pos = pos_ref[:, mine].astype(F32)
    by_row = [jnp.broadcast_to(pos[s : s + 1], (HALF, HEAD_DIM)).T for s in range(3)]
    chosen = jnp.where(freq < 16, by_row[0], jnp.where(freq < 40, by_row[1], by_row[2]))
    angle = chosen * jnp.exp(freq.astype(F32) * (-2.0 * math.log(1e6) / HEAD_DIM))
    sine = jnp.sin(angle)
    cos_ref[...] = jnp.cos(angle)
    sin_ref[...] = jnp.where(lane < HEAD_DIM // 2, -sine, sine)

    acc[...] = jnp.broadcast_to(mbias_ref[...], acc.shape)
    kv_pass(0)
    w_wait(CROSS_DOWN, 1)
    w_sibling(CROSS_DOWN)
    w_wait(CROSS_UP, 0)
    w_sibling(CROSS_UP)
    for slot in (0, NEXT_DOWN, NEXT_UP, FAR):
        w_sibling_wait(slot)
    merge(4, lambda i: hi * 4 + i)
    kv_pass(1)
    for half in (0, 1):
        w_wait(CROSS_FAR, half)
        w_sibling(CROSS_FAR, half)
    for slot in (CROSS, CROSS_DOWN, CROSS_UP):
        w_sibling_wait(slot)
    merge(3, lambda i: (1 - hi) * 4 + lax.rem(y + i + 3, 4))
    kv_pass(2)
    for half in (0, 1):
        w_sibling_wait(CROSS_FAR, half)
    merge(1, lambda i: (1 - hi) * 4 + lax.rem(y + 2, 4))

    visual[...] = acc[...].astype(BF16)
    partner = (g, 1 - roll, z)
    send(visual.at[theirs], xs.at[roll], v_sem.at[0], v_sem.at[1], partner)
    xs[roll] = visual[mine, :]
    for group in range(3):
        kv_end(group)
    arrived(xs.at[1 - roll], v_sem.at[1])

    total = jnp.zeros((HALF, 1), F32)
    for r in range(2):
        start = pl.multiple_of(r * 4096 + z * COLS, COLS)
        v = xs[r].astype(F32)
        total += jnp.sum(v * v, axis=1, keepdims=True)
        xg[r] = (v * gain_ref[:, pl.ds(start, COLS)]).astype(BF16)
    sumsq[...] = jnp.broadcast_to(total, (HALF, HALF)).T[:8]

    def product(j):
        return jnp.dot(xg[0], kvbuf[j, :COLS], preferred_element_type=F32) + jnp.dot(
            xg[1], kvbuf[j, COLS:], preferred_element_type=F32
        )

    def partial_copies(j):
        sign = 2 * lax.rem(j, 2) - 1
        device = at(dz=(j + 1) // 2 * sign)
        back = j + sign * (1 - j // 7)
        return [
            pltpu.make_async_remote_copy(
                src_ref=src,
                dst_ref=dst.at[back],
                send_sem=ssem.at[j],
                recv_sem=rsem.at[back],
                device_id=device,
                device_id_type=MESH,
            )
            for src, dst, ssem, rsem in (
                (sumsq, sumsq_in, q_send, q_recv),
                (sbuf.at[j], rbuf, p_send, p_recv),
            )
        ]

    def partial_step(i, carry):
        j = 7 - i
        copies = partial_copies(j)
        copies[0].start()
        sbuf[j] = product(j).astype(BF16)
        copies[1].start()
        return carry

    lax.fori_loop(0, 7, partial_step, 0)
    proj[...] = product(0)

    def total_step(j, square):
        arrived(sumsq_in.at[j], q_recv.at[j])
        arrived(rbuf.at[j], p_recv.at[j])
        proj[...] += rbuf[j].astype(F32)
        return square + sumsq_in[j]

    square = lax.fori_loop(1, 8, total_step, sumsq[...])
    inv = lax.rsqrt(square * (1.0 / 8192.0) + 1e-06)
    inv = jnp.broadcast_to(inv[:1], (HALF, HALF)).T
    key = proj[:, :HEAD_DIM] * inv + kvbias_ref[:, :HEAD_DIM]
    value = proj[:, HEAD_DIM:] * inv + kvbias_ref[:, HEAD_DIM:]
    key = key * cos_ref[...] + pltpu.roll(key, HEAD_DIM // 2, 1) * sin_ref[...]
    res[:, :HEAD_DIM] = key.astype(BF16)
    res[:, HEAD_DIM:] = value.astype(BF16)
    send(res, res_in, o_sem.at[0], o_sem.at[1], partner)
    out_ref[mine, :] = res[...]
    arrived(res_in, o_sem.at[1])
    out_ref[theirs, :] = res_in[...]
    for copy in started:
        copy.wait_send()

    def sent_step(j, carry):
        for copy in partial_copies(j):
            copy.wait_send()
        return carry

    lax.fori_loop(1, 8, sent_step, 0)


def gather_project(vis, w, kvw, mbias, gain, kvbias, pos):
    vmem = pl.BlockSpec(memory_space=pltpu.VMEM)
    hbm = pl.BlockSpec(memory_space=pltpu.HBM)
    dma = pltpu.SemaphoreType.DMA
    return pl.pallas_call(
        gather_project_kernel,
        out_shape=jax.ShapeDtypeStruct((ROWS, 2 * HEAD_DIM), BF16),
        in_specs=[hbm] * 7,
        out_specs=vmem,
        scratch_shapes=[
            pltpu.VMEM((1, COLS), F32),
            pltpu.VMEM((1, 8192), F32),
            pltpu.VMEM((1, 2 * HEAD_DIM), F32),
            pltpu.VMEM((3, ROWS), jnp.int32),
            pltpu.VMEM((HALF, HEAD_DIM), F32),
            pltpu.VMEM((HALF, HEAD_DIM), F32),
            pltpu.VMEM((ROWS, 5120), BF16),
            pltpu.VMEM((8, ROWS, PAIR), BF16),
            pltpu.VMEM((8, PAIR, COLS), BF16),
            pltpu.VMEM((8, 1024, 2 * HEAD_DIM), BF16),
            pltpu.VMEM((ROWS, COLS), F32),
            pltpu.VMEM((ROWS, COLS), BF16),
            pltpu.VMEM((2, HALF, COLS), BF16),
            pltpu.VMEM((2, HALF, COLS), BF16),
            pltpu.VMEM((8, HALF), F32),
            pltpu.VMEM((8, 8, HALF), F32),
            pltpu.VMEM((8, HALF, 2 * HEAD_DIM), BF16),
            pltpu.VMEM((8, HALF, 2 * HEAD_DIM), BF16),
            pltpu.VMEM((HALF, 2 * HEAD_DIM), F32),
            pltpu.VMEM((HALF, 2 * HEAD_DIM), BF16),
            pltpu.VMEM((HALF, 2 * HEAD_DIM), BF16),
            dma((7,)),
            dma((32,)),
            dma((32,)),
            dma((8,)),
            dma((8,)),
            dma((12,)),
            dma((12,)),
            dma((2,)),
            dma((8,)),
            dma((8,)),
            dma((8,)),
            dma((8,)),
            dma((2,)),
        ],
        compiler_params=pltpu.CompilerParams(
            collective_id=0, has_side_effects=True, vmem_limit_bytes=64 * 2**20
        ),
        cost_estimate=pl.CostEstimate(
            flops=2_500_000_000, bytes_accessed=8_000_000, transcendentals=1_500_000
        ),
        name="gather_project",
    )(vis, w, kvw, mbias, gain, kvbias, pos)


def attention_kernel(
    count_ref,
    length_ref,
    q_hbm,
    tkv_hbm,
    kv_hbm,
    out_hbm,
    q_in,
    tkv_in,
    kv_in,
    out,
    keys,
    values,
    kv_sem,
    tkv_sem,
    q_sem,
    out_sem,
):
    rollouts = q_in.shape[0]
    kv_copy = pltpu.make_async_copy(kv_hbm, kv_in, kv_sem)
    kv_copy.start()

    def load(r, carry):
        rows = pl.ds(pl.multiple_of(r * RLEN, RLEN), RLEN)
        pltpu.make_async_copy(tkv_hbm.at[rows], tkv_in.at[r], tkv_sem.at[r]).start()
        pltpu.make_async_copy(q_hbm.at[rows], q_in.at[r], q_sem.at[r]).start()
        return carry

    lax.fori_loop(0, rollouts, load, 0)

    kv_copy.wait()
    live = lax.broadcasted_iota(jnp.int32, (ROWS, HEAD_DIM), 0) < count_ref[0]
    image_keys = kv_in[:, :HEAD_DIM]
    image_keys = jnp.where(live, image_keys, image_keys[:1])
    image_values = jnp.where(live, kv_in[:, HEAD_DIM:], 0.0).astype(BF16)
    keys[...] = image_keys
    values[:, :HEAD_DIM] = image_values
    values[:, HEAD_DIM:] = jnp.where(live, 1.0, 0.0).astype(BF16)

    batch = BATCH * RLEN
    token = lax.rem(lax.broadcasted_iota(jnp.int32, (batch, RLEN), 0), RLEN)
    causal = lax.broadcasted_iota(jnp.int32, (batch, RLEN), 1) <= token
    factor = HEAD_DIM ** (-0.5) * math.log2(math.e)
    def one(r):
        rows = pl.ds(pl.multiple_of(r * RLEN, RLEN), RLEN)
        text_keys = tkv_in[r, :, :HEAD_DIM]
        text_values = jnp.concatenate(
            [tkv_in[r, :, HEAD_DIM:], jnp.ones((RLEN, HEAD_DIM), BF16)], axis=1
        )
        kept = token < length_ref[r]
        for h in range(0, 8, BATCH):
            heads = [slice(k * HEAD_DIM, (k + 1) * HEAD_DIM) for k in range(h, h + BATCH)]
            q = jnp.concatenate([q_in[r, :, cols] for cols in heads], axis=0)
            image = lax.dot_general(
                q, keys[...], (((1,), (1,)), ((), ())), preferred_element_type=F32
            )
            text = lax.dot_general(
                q, text_keys, (((1,), (1,)), ((), ())), preferred_element_type=F32
            )
            text = jnp.where(causal, text, -1e30)
            highest = jnp.maximum(
                jnp.maximum(image[:, :HEAD_DIM], image[:, HEAD_DIM:]), text
            )
            highest = jnp.max(highest, axis=1, keepdims=True)
            image = jnp.exp2((image - highest) * factor).astype(BF16)
            text = jnp.exp2((text - highest) * factor).astype(BF16)
            sums = jnp.dot(image, values[...], preferred_element_type=F32)
            sums += jnp.dot(text, text_values, preferred_element_type=F32)
            attended = jnp.where(kept, sums[:, :HEAD_DIM] / sums[:, HEAD_DIM:], 0.0).astype(BF16)
            for i, cols in enumerate(heads):
                out[r, :, cols] = attended[i * RLEN : (i + 1) * RLEN]

    def rollout(step, carry):
        for i in range(UNROLL):
            r = step * UNROLL + i
            rows = pl.ds(pl.multiple_of(r * RLEN, RLEN), RLEN)
            pltpu.make_async_copy(tkv_hbm.at[rows], tkv_in.at[r], tkv_sem.at[r]).wait()
            pltpu.make_async_copy(q_hbm.at[rows], q_in.at[r], q_sem.at[r]).wait()
        for i in range(UNROLL):
            one(step * UNROLL + i)
        for i in range(UNROLL):
            r = step * UNROLL + i
            rows = pl.ds(pl.multiple_of(r * RLEN, RLEN), RLEN)
            pltpu.make_async_copy(out.at[r], out_hbm.at[rows], out_sem.at[r]).start()
        return carry

    lax.fori_loop(0, rollouts // UNROLL, rollout, 0)

    def stored(r, carry):
        rows = pl.ds(pl.multiple_of(r * RLEN, RLEN), RLEN)
        pltpu.make_async_copy(out.at[r], out_hbm.at[rows], out_sem.at[r]).wait()
        return carry

    lax.fori_loop(0, rollouts, stored, 0)


def attention(count, length, q, tkv, kv):
    rollouts = length.shape[0]
    smem = pl.BlockSpec(memory_space=pltpu.SMEM)
    hbm = pl.BlockSpec(memory_space=pl.ANY)
    dma = pltpu.SemaphoreType.DMA
    return pl.pallas_call(
        attention_kernel,
        in_specs=[smem, smem, hbm, hbm, hbm],
        out_specs=hbm,
        out_shape=jax.ShapeDtypeStruct(q.shape, BF16),
        scratch_shapes=[
            pltpu.VMEM((rollouts, RLEN, q.shape[1]), BF16),
            pltpu.VMEM((rollouts, RLEN, tkv.shape[1]), BF16),
            pltpu.VMEM(kv.shape, BF16),
            pltpu.VMEM((rollouts, RLEN, q.shape[1]), BF16),
            pltpu.VMEM((ROWS, HEAD_DIM), BF16),
            pltpu.VMEM((ROWS, 2 * HEAD_DIM), BF16),
            dma,
            dma((rollouts,)),
            dma((rollouts,)),
            dma((rollouts,)),
        ],
        compiler_params=pltpu.CompilerParams(vmem_limit_bytes=64 * 2**20),
        name="attention",
    )(count, length, q, tkv, kv)


def body(
    vis_hidden,
    merge_weight,
    merge_bias,
    norm_gain,
    kv_weight,
    kv_bias,
    queries,
    text_kv,
    image_count,
    image_pos,
    resp_length,
):
    kv = gather_project(
        vis_hidden,
        merge_weight,
        kv_weight,
        merge_bias.reshape(1, -1),
        norm_gain.reshape(1, -1),
        kv_bias.reshape(1, -1),
        image_pos,
    )
    return attention(image_count, resp_length, queries, text_kv, kv)


def solution(mesh):
    in_specs = (
        P("group", None),
        P("group", ("roll", "tp")),
        P(("roll", "tp")),
        P(),
        P(None, "tp"),
        P("tp"),
        P(("group", "roll"), "tp"),
        P(("group", "roll"), "tp"),
        P("group"),
        P(None, "group"),
        P(("group", "roll")),
    )
    out_specs = P(("group", "roll"), "tp")
    return jax.shard_map(body, mesh=mesh, in_specs=in_specs, out_specs=out_specs, check_vma=False)
```

```python
import math

import jax
import jax.numpy as jnp
from jax import lax
from jax.experimental import pallas as pl
from jax.experimental.pallas import tpu as pltpu
from jax.sharding import PartitionSpec as P

HEAD_DIM = 128
RLEN = 128
BATCH = 8
UNROLL = 4
MESH = pl.DeviceIdType.MESH
BF16 = jnp.bfloat16
F32 = jnp.float32

ZOFF = (0, 1, -1, 2, -2, 3, -3, 4)
ZBACK = (0, 2, 1, 4, 3, 6, 5, 7)
KVGROUPS = ((0, 3), (3, 2), (5, 2))
FAR_SLOT = 7
SLOTS = [(0, 0), (0, 1), (0, -1), (1, 0), (0, 2), (1, 1), (1, -1), (1, 2)]
NEXT_UP, NEXT_DOWN, CROSS, FAR, CROSS_UP, CROSS_DOWN, CROSS_FAR = range(1, 8)
ROWS = 256
HALF = 128
HID = 320
PAIR = 640
COLS = 512


def gather_project_kernel(
    vis_hbm,
    w_hbm,
    kvw_hbm,
    mbias_hbm,
    gain_hbm,
    kvbias_hbm,
    pos_hbm,
    out_ref,
    mbias_ref,
    gain_ref,
    kvbias_ref,
    pos_ref,
    cos_ref,
    sin_ref,
    vis,
    act,
    wbuf,
    kvbuf,
    acc,
    visual,
    xs,
    xg,
    sumsq,
    sumsq_in,
    sbuf,
    rbuf,
    proj,
    res,
    res_in,
    local_sem,
    w_send,
    w_recv,
    kz_send,
    kz_recv,
    kx_send,
    kx_recv,
    v_sem,
    q_send,
    q_recv,
    p_send,
    p_recv,
    o_sem,
):
    g = lax.axis_index("group")
    roll = lax.axis_index("roll")
    z = lax.axis_index("tp")
    hi = g // 8
    y = lax.rem(g // 2, 4)
    core = lax.rem(g, 2)
    x = 2 * hi + roll
    me_k = hi * 4 + y

    def at(dx=0, dy=0, dz=0, sib=False):
        xx = lax.rem(x + dx + 4, 4)
        yy = lax.rem(y + dy + 4, 4)
        zz = lax.rem(z + dz + 8, 8)
        cc = 1 - core if sib else core
        return ((xx // 2) * 8 + yy * 2 + cc, lax.rem(xx, 2), zz)

    def k_of(dh, dy):
        hh = 1 - hi if dh else hi
        return hh * 4 + lax.rem(y + dy + 4, 4)

    started = []

    def send(src, dst, ssem, rsem, device):
        copy = pltpu.make_async_remote_copy(
            src_ref=src,
            dst_ref=dst,
            send_sem=ssem,
            recv_sem=rsem,
            device_id=device,
            device_id_type=MESH,
        )
        copy.start()
        started.append(copy)

    def arrived(dst, rsem):
        pltpu.make_async_remote_copy(
            src_ref=dst,
            dst_ref=dst,
            send_sem=rsem,
            recv_sem=rsem,
            device_id=at(sib=True),
            device_id_type=MESH,
        ).wait_recv()

    part_start = roll * COLS + core * ROWS

    def kv_piece(first, count, start, rows):
        return kvbuf.at[pl.ds(first, count), pl.ds(pl.multiple_of(start, HALF), rows)]

    def kv_rows(zz):
        start = roll * 4096 + zz * COLS + core * ROWS
        return pl.ds(pl.multiple_of(start, ROWS), ROWS)

    quarter = x * 2 + core

    def far_rows(zz):
        start = (quarter // 4) * 4096 + zz * COLS + lax.rem(quarter, 4) * HALF
        return pl.ds(pl.multiple_of(start, HALF), HALF)

    def far_piece(part):
        return kvbuf.at[FAR_SLOT, pl.ds(pl.multiple_of(part * HALF, HALF), HALF)]

    def kv_slot(j):
        return kvbuf.at[j, pl.ds(pl.multiple_of(part_start, ROWS), ROWS)]

    def w_piece(slot, half, cc):
        dh, dy = SLOTS[slot]
        start, rows = (0, HID) if half is None else (half * (HID // 2), HID // 2)
        return wbuf.at[k_of(dh, dy), pl.ds(pl.multiple_of(cc * HID + start, 32), rows)]

    own_w = pltpu.make_async_copy(w_hbm, w_piece(0, None, core), local_sem.at[0])
    own_kv = pltpu.make_async_copy(kvw_hbm.at[kv_rows(z)], kv_slot(0), local_sem.at[1])
    own_vis = pltpu.make_async_copy(vis_hbm, vis, local_sem.at[2])
    own_w.start()
    own_kv.start()
    own_vis.start()
    small = [
        pltpu.make_async_copy(src, dst, local_sem.at[3 + i])
        for i, (src, dst) in enumerate(
            (
                (mbias_hbm, mbias_ref),
                (gain_hbm, gain_ref),
                (kvbias_hbm, kvbias_ref),
                (pos_hbm, pos_ref),
            )
        )
    ]
    for copy in small:
        copy.start()

    partners = [at(dx=1), at(dx=-1), at(dx=2), at(dy=1), at(dy=-1), at(dy=2), at(sib=True)]
    partners += [at(dz=d) for d in ZOFF[1:]]
    barrier = pltpu.get_barrier_semaphore()
    for partner in partners:
        pl.semaphore_signal(barrier, inc=1, device_id=partner, device_id_type=MESH)
    pl.semaphore_wait(barrier, len(partners))

    sent = iter(range(64))
    kx_sent = iter(range(64))

    def w_send_to(slot, half, dx=0, dy=0):
        dh, ddy = SLOTS[slot]
        there = SLOTS.index(((dh + (1 if dx else 0)) % 2, (ddy - dy + 1) % 4 - 1))
        block = w_piece(slot, half, core)
        send(block, block, w_send.at[next(sent)], w_recv.at[there * 2 + half], at(dx=dx, dy=dy))

    def w_wait(slot, half):
        arrived(w_piece(slot, half, core), w_recv.at[slot * 2 + half])

    def w_sibling(slot, half=None):
        block = w_piece(slot, half, core)
        index = 16 + slot * 2 + (half or 0)
        send(block, block, w_send.at[next(sent)], w_recv.at[index], at(sib=True))

    def w_sibling_wait(slot, half=None):
        arrived(w_piece(slot, half, 1 - core), w_recv.at[16 + slot * 2 + (half or 0)])

    own_w.wait()
    for half in (0, 1):
        w_send_to(0, half, dx=2)
    for j in (1, 2, 3, 4, 5, 6):
        zz = lax.rem(z + ZOFF[j] + 8, 8)
        send(
            kvw_hbm.at[kv_rows(zz)],
            kv_slot(ZBACK[j]),
            kz_send.at[j],
            kz_recv.at[ZBACK[j]],
            at(dz=ZOFF[j]),
        )
    send(
        kvw_hbm.at[far_rows(lax.rem(z + 4, 8))],
        far_piece(quarter),
        kz_send.at[FAR_SLOT],
        kz_recv.at[FAR_SLOT],
        at(dz=4),
    )
    for half in (0, 1):
        w_send_to(0, half, dy=1)
        w_send_to(0, 1 - half, dy=-1)
    w_sibling(0)

    own_vis.wait()

    def activate(k):
        def step(i, carry):
            rows = pl.ds(pl.multiple_of(i * 32, 32), 32)
            v = vis[rows, k * PAIR : (k + 1) * PAIR].astype(F32)
            act[k, rows] = (v * (1.0 + lax.erf(v * (1.0 / math.sqrt(2.0)))) * 0.5).astype(BF16)
            return carry

        lax.fori_loop(0, ROWS // 32, step, 0)

    def merge(count, chip):
        def step(i, carry):
            k = chip(i)
            acc[...] += jnp.dot(act[k], wbuf[k], preferred_element_type=F32)
            return carry

        lax.fori_loop(0, count, step, 0)

    def kv_share(group):
        first, count = KVGROUPS[group]
        for j in range(first, first + count):
            if j:
                arrived(kv_slot(j), kz_recv.at[j])
        for i, dx in ((0, 1), (1, -1)):
            block = kv_piece(first, count, part_start + i * HALF, HALF)
            send(block, block, kx_send.at[next(kx_sent)], kx_recv.at[group * 4 + i], at(dx=dx))
        block = kv_piece(first, count, part_start, ROWS)
        send(block, block, kx_send.at[next(kx_sent)], kx_recv.at[group * 4 + 2], at(sib=True))

    other_start = (1 - roll) * COLS + core * ROWS

    def kv_pass(group):
        first, count = KVGROUPS[group]
        for i in (0, 1):
            block = kv_piece(first, count, other_start + i * HALF, HALF)
            arrived(block, kx_recv.at[group * 4 + i])
        block = kv_piece(first, count, other_start, ROWS)
        send(block, block, kx_send.at[next(kx_sent)], kx_recv.at[group * 4 + 3], at(sib=True))

    far_sources = ((1, 13), (-1, 14), (2, 15))

    def far_at(dx, cc):
        return far_piece(lax.rem(x + dx + 4, 4) * 2 + cc)

    def far_share():
        block = far_piece(quarter)
        arrived(block, kz_recv.at[FAR_SLOT])
        for dx, index in ((2, 15), (1, 14), (-1, 13)):
            send(block, block, kx_send.at[next(kx_sent)], kx_recv.at[index], at(dx=dx))
        send(block, block, kx_send.at[next(kx_sent)], kx_recv.at[12], at(sib=True))

    def far_pass():
        for dx, index in far_sources:
            block = far_at(dx, core)
            arrived(block, kx_recv.at[index])
            send(block, block, kx_send.at[next(kx_sent)], kx_recv.at[index + 3], at(sib=True))

    def far_end():
        arrived(far_at(0, 1 - core), kx_recv.at[12])
        for dx, index in far_sources:
            arrived(far_at(dx, 1 - core), kx_recv.at[index + 3])

    def kv_end(group):
        first, count = KVGROUPS[group]
        for i, rr in ((2, roll), (3, 1 - roll)):
            block = kv_piece(first, count, rr * COLS + (1 - core) * ROWS, ROWS)
            arrived(block, kx_recv.at[group * 4 + i])

    activate(0)
    activate(1)
    w_wait(NEXT_DOWN, 0)
    w_send_to(NEXT_DOWN, 0, dy=1)
    w_wait(NEXT_UP, 1)
    w_send_to(NEXT_UP, 1, dy=-1)
    activate(2)
    for half in (0, 1):
        w_wait(CROSS, half)
        w_send_to(CROSS, half, dy=1)
        w_send_to(CROSS, half, dy=-1)
        activate(3 + half)
    own_kv.wait()
    kv_share(0)
    w_sibling(CROSS)
    w_wait(NEXT_DOWN, 1)
    w_sibling(NEXT_DOWN)
    w_wait(NEXT_UP, 0)
    w_sibling(NEXT_UP)
    activate(5)
    kv_share(1)
    w_wait(CROSS_DOWN, 0)
    w_send_to(CROSS_DOWN, 0, dy=1)
    w_wait(CROSS_UP, 1)
    w_send_to(CROSS_UP, 1, dy=-1)
    activate(6)
    for half in (0, 1):
        w_wait(FAR, half)
    w_sibling(FAR)
    kv_share(2)
    far_share()
    activate(7)
    for copy in small:
        copy.wait()
    mine = pl.ds(pl.multiple_of(roll * HALF, HALF), HALF)
    theirs = pl.ds(pl.multiple_of((1 - roll) * HALF, HALF), HALF)
    lane = lax.broadcasted_iota(jnp.int32, (HALF, HEAD_DIM), 1)
    freq = lax.rem(lane, HEAD_DIM // 2)
    pos = pos_ref[:, mine].astype(F32)
    by_row = [jnp.broadcast_to(pos[s : s + 1], (HALF, HEAD_DIM)).T for s in range(3)]
    chosen = jnp.where(freq < 16, by_row[0], jnp.where(freq < 40, by_row[1], by_row[2]))
    angle = chosen * jnp.exp(freq.astype(F32) * (-2.0 * math.log(1e6) / HEAD_DIM))
    sine = jnp.sin(angle)
    cos_ref[...] = jnp.cos(angle)
    sin_ref[...] = jnp.where(lane < HEAD_DIM // 2, -sine, sine)

    acc[...] = jnp.broadcast_to(mbias_ref[...], acc.shape)
    kv_pass(0)
    w_wait(CROSS_DOWN, 1)
    w_sibling(CROSS_DOWN)
    w_wait(CROSS_UP, 0)
    w_sibling(CROSS_UP)
    for slot in (0, NEXT_DOWN, NEXT_UP, FAR):
        w_sibling_wait(slot)
    merge(4, lambda i: hi * 4 + i)
    kv_pass(1)
    for half in (0, 1):
        w_wait(CROSS_FAR, half)
        w_sibling(CROSS_FAR, half)
    for slot in (CROSS, CROSS_DOWN, CROSS_UP):
        w_sibling_wait(slot)
    merge(3, lambda i: (1 - hi) * 4 + lax.rem(y + i + 3, 4))
    kv_pass(2)
    far_pass()
    for half in (0, 1):
        w_sibling_wait(CROSS_FAR, half)
    merge(1, lambda i: (1 - hi) * 4 + lax.rem(y + 2, 4))

    visual[...] = acc[...].astype(BF16)
    partner = (g, 1 - roll, z)
    send(visual.at[theirs], xs.at[roll], v_sem.at[0], v_sem.at[1], partner)
    xs[roll] = visual[mine, :]
    for group in range(3):
        kv_end(group)
    far_end()
    arrived(xs.at[1 - roll], v_sem.at[1])

    total = jnp.zeros((HALF, 1), F32)
    for r in range(2):
        start = pl.multiple_of(r * 4096 + z * COLS, COLS)
        v = xs[r].astype(F32)
        total += jnp.sum(v * v, axis=1, keepdims=True)
        xg[r] = (v * gain_ref[:, pl.ds(start, COLS)]).astype(BF16)
    sumsq[...] = jnp.broadcast_to(total, (HALF, HALF)).T[:8]

    def product(j):
        return jnp.dot(xg[0], kvbuf[j, :COLS], preferred_element_type=F32) + jnp.dot(
            xg[1], kvbuf[j, COLS:], preferred_element_type=F32
        )

    def sumsq_copy(j):
        sign = 2 * lax.rem(j, 2) - 1
        back = j + sign * (1 - j // 7)
        return pltpu.make_async_remote_copy(
            src_ref=sumsq,
            dst_ref=sumsq_in.at[back],
            send_sem=q_send.at[j],
            recv_sem=q_recv.at[back],
            device_id=at(dz=(j + 1) // 2 * sign),
            device_id_type=MESH,
        )

    def sumsq_send(i, carry):
        sumsq_copy(i).start()
        return carry

    lax.fori_loop(1, 8, sumsq_send, 0)

    way = 1 - 2 * core

    def ahead(k):
        return 2 * k - 1 + core

    def behind(k):
        return 2 * k - core

    def partial_send(j, dst, slot, steps):
        send(sbuf.at[j], dst.at[slot], p_send.at[j], p_recv.at[slot], at(dz=way * steps))

    sbuf[7] = product(7).astype(BF16)
    partial_send(7, rbuf, 7, 1)
    sbuf[behind(3)] = product(behind(3)).astype(BF16)
    partial_send(behind(3), rbuf, 0, -1)
    sbuf[ahead(2)] = product(ahead(2)).astype(BF16)
    partial_send(ahead(2), rbuf, behind(2), 2)
    sbuf[ahead(1)] = product(ahead(1)).astype(BF16)
    partial_send(ahead(1), rbuf, behind(1), 1)
    sbuf[behind(1)] = product(behind(1)).astype(BF16)
    partial_send(behind(1), rbuf, ahead(1), -1)
    proj[...] = product(ahead(3))
    arrived(rbuf.at[7], p_recv.at[7])
    sbuf[ahead(3)] = (proj[...] + rbuf[7].astype(F32)).astype(BF16)
    partial_send(ahead(3), rbuf, behind(3), 3)
    proj[...] = product(behind(2))
    arrived(rbuf.at[0], p_recv.at[0])
    sbuf[behind(2)] = (proj[...] + rbuf[0].astype(F32)).astype(BF16)
    partial_send(behind(2), rbuf, ahead(2), -2)
    proj[...] = product(0)

    def square_step(j, square):
        arrived(sumsq_in.at[j], q_recv.at[j])
        return square + sumsq_in[j]

    square = lax.fori_loop(1, 8, square_step, sumsq[...])
    inv = lax.rsqrt(square * (1.0 / 8192.0) + 1e-06)
    inv = jnp.broadcast_to(inv[:1], (HALF, HALF)).T
    for slot in (ahead(1), behind(1), behind(2), ahead(2), behind(3)):
        arrived(rbuf.at[slot], p_recv.at[slot])
        proj[...] += rbuf[slot].astype(F32)
    key = proj[:, :HEAD_DIM] * inv + kvbias_ref[:, :HEAD_DIM]
    value = proj[:, HEAD_DIM:] * inv + kvbias_ref[:, HEAD_DIM:]
    key = key * cos_ref[...] + pltpu.roll(key, HEAD_DIM // 2, 1) * sin_ref[...]
    res[:, :HEAD_DIM] = key.astype(BF16)
    res[:, HEAD_DIM:] = value.astype(BF16)
    send(res, res_in, o_sem.at[0], o_sem.at[1], partner)
    out_ref[mine, :] = res[...]
    arrived(res_in, o_sem.at[1])
    out_ref[theirs, :] = res_in[...]
    for copy in started:
        copy.wait_send()

    def sent_step(j, carry):
        sumsq_copy(j).wait_send()
        return carry

    lax.fori_loop(1, 8, sent_step, 0)


def gather_project(vis, w, kvw, mbias, gain, kvbias, pos):
    vmem = pl.BlockSpec(memory_space=pltpu.VMEM)
    hbm = pl.BlockSpec(memory_space=pltpu.HBM)
    dma = pltpu.SemaphoreType.DMA
    return pl.pallas_call(
        gather_project_kernel,
        out_shape=jax.ShapeDtypeStruct((ROWS, 2 * HEAD_DIM), BF16),
        in_specs=[hbm] * 7,
        out_specs=vmem,
        scratch_shapes=[
            pltpu.VMEM((1, COLS), F32),
            pltpu.VMEM((1, 8192), F32),
            pltpu.VMEM((1, 2 * HEAD_DIM), F32),
            pltpu.VMEM((3, ROWS), jnp.int32),
            pltpu.VMEM((HALF, HEAD_DIM), F32),
            pltpu.VMEM((HALF, HEAD_DIM), F32),
            pltpu.VMEM((ROWS, 5120), BF16),
            pltpu.VMEM((8, ROWS, PAIR), BF16),
            pltpu.VMEM((8, PAIR, COLS), BF16),
            pltpu.VMEM((8, 1024, 2 * HEAD_DIM), BF16),
            pltpu.VMEM((ROWS, COLS), F32),
            pltpu.VMEM((ROWS, COLS), BF16),
            pltpu.VMEM((2, HALF, COLS), BF16),
            pltpu.VMEM((2, HALF, COLS), BF16),
            pltpu.VMEM((8, HALF), F32),
            pltpu.VMEM((8, 8, HALF), F32),
            pltpu.VMEM((8, HALF, 2 * HEAD_DIM), BF16),
            pltpu.VMEM((8, HALF, 2 * HEAD_DIM), BF16),
            pltpu.VMEM((HALF, 2 * HEAD_DIM), F32),
            pltpu.VMEM((HALF, 2 * HEAD_DIM), BF16),
            pltpu.VMEM((HALF, 2 * HEAD_DIM), BF16),
            dma((7,)),
            dma((32,)),
            dma((32,)),
            dma((8,)),
            dma((8,)),
            dma((19,)),
            dma((19,)),
            dma((2,)),
            dma((8,)),
            dma((8,)),
            dma((8,)),
            dma((8,)),
            dma((2,)),
        ],
        compiler_params=pltpu.CompilerParams(
            collective_id=0, has_side_effects=True, vmem_limit_bytes=60 * 2**20
        ),
        cost_estimate=pl.CostEstimate(
            flops=2_500_000_000, bytes_accessed=8_000_000, transcendentals=1_500_000
        ),
        name="gather_project",
    )(vis, w, kvw, mbias, gain, kvbias, pos)


def attention_kernel(
    count_ref,
    length_ref,
    q_in,
    tkv_in,
    kv_in,
    out_hbm,
    out,
    keys,
    values,
    out_sem,
):
    rollouts = length_ref.shape[0]
    live = lax.broadcasted_iota(jnp.int32, (ROWS, HEAD_DIM), 0) < count_ref[0]
    image_keys = kv_in[:, :HEAD_DIM]
    image_keys = jnp.where(live, image_keys, image_keys[:1])
    image_values = jnp.where(live, kv_in[:, HEAD_DIM:], 0.0).astype(BF16)
    keys[...] = image_keys
    values[:, :HEAD_DIM] = image_values
    values[:, HEAD_DIM:] = jnp.where(live, 1.0, 0.0).astype(BF16)

    batch = BATCH * RLEN
    token = lax.rem(lax.broadcasted_iota(jnp.int32, (batch, RLEN), 0), RLEN)
    causal = lax.broadcasted_iota(jnp.int32, (batch, RLEN), 1) <= token
    factor = HEAD_DIM ** (-0.5) * math.log2(math.e)
    def one(r):
        rows = pl.ds(pl.multiple_of(r * RLEN, RLEN), RLEN)
        text_keys = tkv_in[rows, :HEAD_DIM]
        text_values = jnp.concatenate(
            [tkv_in[rows, HEAD_DIM:], jnp.ones((RLEN, HEAD_DIM), BF16)], axis=1
        )
        kept = token < length_ref[r]
        for h in range(0, 8, BATCH):
            heads = [slice(k * HEAD_DIM, (k + 1) * HEAD_DIM) for k in range(h, h + BATCH)]
            q = jnp.concatenate([q_in[rows, cols] for cols in heads], axis=0)
            image = lax.dot_general(
                q, keys[...], (((1,), (1,)), ((), ())), preferred_element_type=F32
            )
            text = lax.dot_general(
                q, text_keys, (((1,), (1,)), ((), ())), preferred_element_type=F32
            )
            text = jnp.where(causal, text, -1e30)
            highest = jnp.maximum(
                jnp.maximum(image[:, :HEAD_DIM], image[:, HEAD_DIM:]), text
            )
            highest = jnp.max(highest, axis=1, keepdims=True)
            image = jnp.exp2((image - highest) * factor).astype(BF16)
            text = jnp.exp2((text - highest) * factor).astype(BF16)
            sums = jnp.dot(image, values[...], preferred_element_type=F32)
            sums += jnp.dot(text, text_values, preferred_element_type=F32)
            attended = jnp.where(kept, sums[:, :HEAD_DIM] / sums[:, HEAD_DIM:], 0.0).astype(BF16)
            for i, cols in enumerate(heads):
                out[r, :, cols] = attended[i * RLEN : (i + 1) * RLEN]

    def rollout(step, carry):
        for i in range(UNROLL):
            one(step * UNROLL + i)
        for i in range(UNROLL):
            r = step * UNROLL + i
            rows = pl.ds(pl.multiple_of(r * RLEN, RLEN), RLEN)
            pltpu.make_async_copy(out.at[r], out_hbm.at[rows], out_sem.at[r]).start()
        return carry

    lax.fori_loop(0, rollouts // UNROLL, rollout, 0)

    def stored(r, carry):
        rows = pl.ds(pl.multiple_of(r * RLEN, RLEN), RLEN)
        pltpu.make_async_copy(out.at[r], out_hbm.at[rows], out_sem.at[r]).wait()
        return carry

    lax.fori_loop(0, rollouts, stored, 0)


def attention(count, length, q, tkv, kv):
    rollouts = length.shape[0]
    smem = pl.BlockSpec(memory_space=pltpu.SMEM)
    vmem = pl.BlockSpec(memory_space=pltpu.VMEM)
    hbm = pl.BlockSpec(memory_space=pl.ANY)
    dma = pltpu.SemaphoreType.DMA
    return pl.pallas_call(
        attention_kernel,
        in_specs=[smem, smem, vmem, vmem, vmem],
        out_specs=hbm,
        out_shape=jax.ShapeDtypeStruct(q.shape, BF16),
        scratch_shapes=[
            pltpu.VMEM((rollouts, RLEN, q.shape[1]), BF16),
            pltpu.VMEM((ROWS, HEAD_DIM), BF16),
            pltpu.VMEM((ROWS, 2 * HEAD_DIM), BF16),
            dma((rollouts,)),
        ],
        compiler_params=pltpu.CompilerParams(vmem_limit_bytes=32 * 2**20),
        name="attention",
    )(count, length, q, tkv, kv)


def body(
    vis_hidden,
    merge_weight,
    merge_bias,
    norm_gain,
    kv_weight,
    kv_bias,
    queries,
    text_kv,
    image_count,
    image_pos,
    resp_length,
):
    kv = gather_project(
        vis_hidden,
        merge_weight,
        kv_weight,
        merge_bias.reshape(1, -1),
        norm_gain.reshape(1, -1),
        kv_bias.reshape(1, -1),
        image_pos,
    )
    return attention(image_count, resp_length, queries, text_kv, kv)


def solution(mesh):
    in_specs = (
        P("group", None),
        P("group", ("roll", "tp")),
        P(("roll", "tp")),
        P(),
        P(None, "tp"),
        P("tp"),
        P(("group", "roll"), "tp"),
        P(("group", "roll"), "tp"),
        P("group"),
        P(None, "group"),
        P(("group", "roll")),
    )
    out_specs = P(("group", "roll"), "tp")
    return jax.shard_map(body, mesh=mesh, in_specs=in_specs, out_specs=out_specs, check_vma=False)
```

```python
import math

import jax
import jax.numpy as jnp
from jax import lax
from jax.experimental import pallas as pl
from jax.experimental.pallas import tpu as pltpu
from jax.sharding import PartitionSpec as P

HEAD_DIM = 128
RLEN = 128
SCORE_FACTOR = HEAD_DIM ** (-0.5) * math.log2(math.e)
UNROLL = 4
MESH = pl.DeviceIdType.MESH
BF16 = jnp.bfloat16
F32 = jnp.float32

ZOFF = (0, 1, -1, 2, -2, 3, -3, 4)
ZBACK = (0, 2, 1, 4, 3, 6, 5, 7)
KVGROUPS = ((0, 3), (3, 2), (5, 2))
FAR_SLOT = 7
SLOTS = [(0, 0), (0, 1), (0, -1), (1, 0), (0, 2), (1, 1), (1, -1), (1, 2)]
NEXT_UP, NEXT_DOWN, CROSS, FAR, CROSS_UP, CROSS_DOWN, CROSS_FAR = range(1, 8)
ROWS = 256
HALF = 128
HID = 320
PAIR = 640
COLS = 512


def gather_project_kernel(
    vis_hbm,
    w_hbm,
    kvw_hbm,
    mbias_hbm,
    gain_hbm,
    kvbias_hbm,
    pos_hbm,
    q_hbm,
    tkv_hbm,
    out_ref,
    text_sums,
    text_max,
    mbias_ref,
    gain_ref,
    kvbias_ref,
    pos_ref,
    cos_ref,
    sin_ref,
    q_in,
    tkv_in,
    vis,
    act,
    wbuf,
    kvbuf,
    acc,
    visual,
    xs,
    xg,
    sumsq,
    sumsq_in,
    sbuf,
    rbuf,
    proj,
    res,
    res_in,
    local_sem,
    w_send,
    w_recv,
    kz_send,
    kz_recv,
    kx_send,
    kx_recv,
    v_sem,
    q_send,
    q_recv,
    p_send,
    p_recv,
    o_sem,
):
    g = lax.axis_index("group")
    roll = lax.axis_index("roll")
    z = lax.axis_index("tp")
    hi = g // 8
    y = lax.rem(g // 2, 4)
    core = lax.rem(g, 2)
    x = 2 * hi + roll
    me_k = hi * 4 + y

    def at(dx=0, dy=0, dz=0, sib=False):
        xx = lax.rem(x + dx + 4, 4)
        yy = lax.rem(y + dy + 4, 4)
        zz = lax.rem(z + dz + 8, 8)
        cc = 1 - core if sib else core
        return ((xx // 2) * 8 + yy * 2 + cc, lax.rem(xx, 2), zz)

    def k_of(dh, dy):
        hh = 1 - hi if dh else hi
        return hh * 4 + lax.rem(y + dy + 4, 4)

    started = []

    def send(src, dst, ssem, rsem, device):
        copy = pltpu.make_async_remote_copy(
            src_ref=src,
            dst_ref=dst,
            send_sem=ssem,
            recv_sem=rsem,
            device_id=device,
            device_id_type=MESH,
        )
        copy.start()
        started.append(copy)

    def arrived(dst, rsem):
        pltpu.make_async_remote_copy(
            src_ref=dst,
            dst_ref=dst,
            send_sem=rsem,
            recv_sem=rsem,
            device_id=at(sib=True),
            device_id_type=MESH,
        ).wait_recv()

    part_start = roll * COLS + core * ROWS

    def kv_piece(first, count, start, rows):
        return kvbuf.at[pl.ds(first, count), pl.ds(pl.multiple_of(start, HALF), rows)]

    def kv_rows(zz):
        start = roll * 4096 + zz * COLS + core * ROWS
        return pl.ds(pl.multiple_of(start, ROWS), ROWS)

    quarter = x * 2 + core

    def far_rows(zz):
        start = (quarter // 4) * 4096 + zz * COLS + lax.rem(quarter, 4) * HALF
        return pl.ds(pl.multiple_of(start, HALF), HALF)

    def far_piece(part):
        return kvbuf.at[FAR_SLOT, pl.ds(pl.multiple_of(part * HALF, HALF), HALF)]

    def kv_slot(j):
        return kvbuf.at[j, pl.ds(pl.multiple_of(part_start, ROWS), ROWS)]

    def w_piece(slot, half, cc):
        dh, dy = SLOTS[slot]
        start, rows = (0, HID) if half is None else (half * (HID // 2), HID // 2)
        return wbuf.at[k_of(dh, dy), pl.ds(pl.multiple_of(cc * HID + start, 32), rows)]

    own_w = pltpu.make_async_copy(w_hbm, w_piece(0, None, core), local_sem.at[0])
    own_kv = pltpu.make_async_copy(kvw_hbm.at[kv_rows(z)], kv_slot(0), local_sem.at[1])
    own_vis = pltpu.make_async_copy(vis_hbm, vis, local_sem.at[2])
    own_w.start()
    own_kv.start()
    own_vis.start()
    small = [
        pltpu.make_async_copy(src, dst, local_sem.at[3 + i])
        for i, (src, dst) in enumerate(
            (
                (mbias_hbm, mbias_ref),
                (gain_hbm, gain_ref),
                (kvbias_hbm, kvbias_ref),
                (pos_hbm, pos_ref),
                (tkv_hbm, tkv_in),
                (q_hbm, q_in),
            )
        )
    ]
    for copy in small:
        copy.start()

    partners = [at(dx=1), at(dx=-1), at(dx=2), at(dy=1), at(dy=-1), at(dy=2), at(sib=True)]
    partners += [at(dz=d) for d in ZOFF[1:]]
    barrier = pltpu.get_barrier_semaphore()
    for partner in partners:
        pl.semaphore_signal(barrier, inc=1, device_id=partner, device_id_type=MESH)
    pl.semaphore_wait(barrier, len(partners))

    sent = iter(range(64))
    kx_sent = iter(range(64))

    def w_send_to(slot, half, dx=0, dy=0):
        dh, ddy = SLOTS[slot]
        there = SLOTS.index(((dh + (1 if dx else 0)) % 2, (ddy - dy + 1) % 4 - 1))
        block = w_piece(slot, half, core)
        send(block, block, w_send.at[next(sent)], w_recv.at[there * 2 + half], at(dx=dx, dy=dy))

    def w_wait(slot, half):
        arrived(w_piece(slot, half, core), w_recv.at[slot * 2 + half])

    def w_sibling(slot, half=None):
        block = w_piece(slot, half, core)
        index = 16 + slot * 2 + (half or 0)
        send(block, block, w_send.at[next(sent)], w_recv.at[index], at(sib=True))

    def w_sibling_wait(slot, half=None):
        arrived(w_piece(slot, half, 1 - core), w_recv.at[16 + slot * 2 + (half or 0)])

    own_w.wait()
    for half in (0, 1):
        w_send_to(0, half, dx=2)
    send(
        kvw_hbm.at[far_rows(lax.rem(z + 4, 8))],
        far_piece(quarter),
        kz_send.at[FAR_SLOT],
        kz_recv.at[FAR_SLOT],
        at(dz=4),
    )
    for j in (1, 2, 3, 4, 5, 6):
        zz = lax.rem(z + ZOFF[j] + 8, 8)
        send(
            kvw_hbm.at[kv_rows(zz)],
            kv_slot(ZBACK[j]),
            kz_send.at[j],
            kz_recv.at[ZBACK[j]],
            at(dz=ZOFF[j]),
        )
    for half in (0, 1):
        w_send_to(0, half, dy=1)
        w_send_to(0, 1 - half, dy=-1)
    w_sibling(0)

    own_vis.wait()

    def activate(k):
        def step(i, carry):
            rows = pl.ds(pl.multiple_of(i * 32, 32), 32)
            v = vis[rows, k * PAIR : (k + 1) * PAIR].astype(F32)
            act[k, rows] = (v * (1.0 + lax.erf(v * (1.0 / math.sqrt(2.0)))) * 0.5).astype(BF16)
            return carry

        lax.fori_loop(0, ROWS // 32, step, 0)

    def merge(count, chip):
        def step(i, carry):
            k = chip(i)
            acc[...] += jnp.dot(act[k], wbuf[k], preferred_element_type=F32)
            return carry

        lax.fori_loop(0, count, step, 0)

    def kv_share(group):
        first, count = KVGROUPS[group]
        for j in range(first, first + count):
            if j:
                arrived(kv_slot(j), kz_recv.at[j])
        for i, dx in ((0, 1), (1, -1)):
            block = kv_piece(first, count, part_start + i * HALF, HALF)
            send(block, block, kx_send.at[next(kx_sent)], kx_recv.at[group * 4 + i], at(dx=dx))
        block = kv_piece(first, count, part_start, ROWS)
        send(block, block, kx_send.at[next(kx_sent)], kx_recv.at[group * 4 + 2], at(sib=True))

    other_start = (1 - roll) * COLS + core * ROWS

    def kv_pass(group):
        first, count = KVGROUPS[group]
        for i in (0, 1):
            block = kv_piece(first, count, other_start + i * HALF, HALF)
            arrived(block, kx_recv.at[group * 4 + i])
        block = kv_piece(first, count, other_start, ROWS)
        send(block, block, kx_send.at[next(kx_sent)], kx_recv.at[group * 4 + 3], at(sib=True))

    far_sources = ((1, 13), (-1, 14), (2, 15))

    def far_at(dx, cc):
        return far_piece(lax.rem(x + dx + 4, 4) * 2 + cc)

    def far_share():
        block = far_piece(quarter)
        arrived(block, kz_recv.at[FAR_SLOT])
        for dx, index in ((2, 15), (1, 14), (-1, 13)):
            send(block, block, kx_send.at[next(kx_sent)], kx_recv.at[index], at(dx=dx))
        send(block, block, kx_send.at[next(kx_sent)], kx_recv.at[12], at(sib=True))

    def far_pass():
        for dx, index in far_sources:
            block = far_at(dx, core)
            arrived(block, kx_recv.at[index])
            send(block, block, kx_send.at[next(kx_sent)], kx_recv.at[index + 3], at(sib=True))

    def far_end():
        arrived(far_at(0, 1 - core), kx_recv.at[12])
        for dx, index in far_sources:
            arrived(far_at(dx, 1 - core), kx_recv.at[index + 3])

    def kv_end(group):
        first, count = KVGROUPS[group]
        for i, rr in ((2, roll), (3, 1 - roll)):
            block = kv_piece(first, count, rr * COLS + (1 - core) * ROWS, ROWS)
            arrived(block, kx_recv.at[group * 4 + i])

    token = lax.rem(lax.broadcasted_iota(jnp.int32, (8 * RLEN, RLEN), 0), RLEN)
    causal = lax.broadcasted_iota(jnp.int32, (8 * RLEN, RLEN), 1) <= token

    def text(first, count):
        def step(r, carry):
            rows = pl.ds(pl.multiple_of(r * RLEN, RLEN), RLEN)
            q = jnp.concatenate(
                [q_in[rows, h * HEAD_DIM : (h + 1) * HEAD_DIM] for h in range(8)], axis=0
            )
            scores = lax.dot_general(
                q,
                tkv_in[rows, :HEAD_DIM],
                (((1,), (1,)), ((), ())),
                preferred_element_type=F32,
            )
            scores = jnp.where(causal, scores, -1e30)
            highest = jnp.max(scores, axis=1, keepdims=True)
            weights = jnp.exp2((scores - highest) * SCORE_FACTOR).astype(BF16)
            values = jnp.concatenate(
                [tkv_in[rows, HEAD_DIM:], jnp.ones((RLEN, HEAD_DIM), BF16)], axis=1
            )
            text_sums[r] = jnp.dot(weights, values, preferred_element_type=F32)
            text_max[r] = jnp.broadcast_to(highest, (8 * RLEN, HEAD_DIM))
            return carry

        lax.fori_loop(first, first + count, step, 0)

    activate(0)
    activate(1)
    for copy in small:
        copy.wait()
    w_wait(NEXT_DOWN, 0)
    w_send_to(NEXT_DOWN, 0, dy=1)
    w_wait(NEXT_UP, 1)
    w_send_to(NEXT_UP, 1, dy=-1)
    activate(2)
    for half in (0, 1):
        w_wait(CROSS, half)
        w_send_to(CROSS, half, dy=1)
        w_send_to(CROSS, half, dy=-1)
        activate(3 + half)
    own_kv.wait()
    kv_share(0)
    w_sibling(CROSS)
    w_wait(NEXT_DOWN, 1)
    w_sibling(NEXT_DOWN)
    w_wait(NEXT_UP, 0)
    w_sibling(NEXT_UP)
    activate(5)
    kv_share(1)
    far_share()
    w_wait(CROSS_DOWN, 0)
    w_send_to(CROSS_DOWN, 0, dy=1)
    w_wait(CROSS_UP, 1)
    w_send_to(CROSS_UP, 1, dy=-1)
    activate(6)
    for half in (0, 1):
        w_wait(FAR, half)
    w_sibling(FAR)
    kv_share(2)
    activate(7)
    mine = pl.ds(pl.multiple_of(roll * HALF, HALF), HALF)
    theirs = pl.ds(pl.multiple_of((1 - roll) * HALF, HALF), HALF)
    lane = lax.broadcasted_iota(jnp.int32, (HALF, HEAD_DIM), 1)
    freq = lax.rem(lane, HEAD_DIM // 2)
    pos = pos_ref[:, mine].astype(F32)
    by_row = [jnp.broadcast_to(pos[s : s + 1], (HALF, HEAD_DIM)).T for s in range(3)]
    chosen = jnp.where(freq < 16, by_row[0], jnp.where(freq < 40, by_row[1], by_row[2]))
    angle = chosen * jnp.exp(freq.astype(F32) * (-2.0 * math.log(1e6) / HEAD_DIM))
    sine = jnp.sin(angle)
    cos_ref[...] = jnp.cos(angle)
    sin_ref[...] = jnp.where(lane < HEAD_DIM // 2, -sine, sine)

    acc[...] = jnp.broadcast_to(mbias_ref[...], acc.shape)
    kv_pass(0)
    w_wait(CROSS_DOWN, 1)
    w_sibling(CROSS_DOWN)
    w_wait(CROSS_UP, 0)
    w_sibling(CROSS_UP)
    for slot in (0, NEXT_DOWN, NEXT_UP, FAR):
        w_sibling_wait(slot)
    merge(4, lambda i: hi * 4 + i)
    kv_pass(1)
    for half in (0, 1):
        w_wait(CROSS_FAR, half)
        w_sibling(CROSS_FAR, half)
    for slot in (CROSS, CROSS_DOWN, CROSS_UP):
        w_sibling_wait(slot)
    merge(3, lambda i: (1 - hi) * 4 + lax.rem(y + i + 3, 4))
    kv_pass(2)
    far_pass()
    for half in (0, 1):
        w_sibling_wait(CROSS_FAR, half)
    merge(1, lambda i: (1 - hi) * 4 + lax.rem(y + 2, 4))

    visual[...] = acc[...].astype(BF16)
    partner = (g, 1 - roll, z)
    send(visual.at[theirs], xs.at[roll], v_sem.at[0], v_sem.at[1], partner)
    xs[roll] = visual[mine, :]
    text(0, 2)
    for group in range(3):
        kv_end(group)
    far_end()
    arrived(xs.at[1 - roll], v_sem.at[1])

    total = jnp.zeros((HALF, 1), F32)
    for r in range(2):
        start = pl.multiple_of(r * 4096 + z * COLS, COLS)
        v = xs[r].astype(F32)
        total += jnp.sum(v * v, axis=1, keepdims=True)
        xg[r] = (v * gain_ref[:, pl.ds(start, COLS)]).astype(BF16)
    sumsq[...] = jnp.broadcast_to(total, (HALF, HALF)).T[:8]

    def product(j):
        return jnp.dot(xg[0], kvbuf[j, :COLS], preferred_element_type=F32) + jnp.dot(
            xg[1], kvbuf[j, COLS:], preferred_element_type=F32
        )

    def sumsq_copy(j):
        sign = 2 * lax.rem(j, 2) - 1
        back = j + sign * (1 - j // 7)
        return pltpu.make_async_remote_copy(
            src_ref=sumsq,
            dst_ref=sumsq_in.at[back],
            send_sem=q_send.at[j],
            recv_sem=q_recv.at[back],
            device_id=at(dz=(j + 1) // 2 * sign),
            device_id_type=MESH,
        )

    def sumsq_send(i, carry):
        sumsq_copy(i).start()
        return carry

    lax.fori_loop(1, 8, sumsq_send, 0)

    way = 1 - 2 * core

    def ahead(k):
        return 2 * k - 1 + core

    def behind(k):
        return 2 * k - core

    def partial_send(j, dst, slot, steps):
        send(sbuf.at[j], dst.at[slot], p_send.at[j], p_recv.at[slot], at(dz=way * steps))

    sbuf[7] = product(7).astype(BF16)
    partial_send(7, rbuf, 7, 1)
    sbuf[behind(3)] = product(behind(3)).astype(BF16)
    partial_send(behind(3), rbuf, 0, -1)
    sbuf[ahead(2)] = product(ahead(2)).astype(BF16)
    partial_send(ahead(2), rbuf, behind(2), 2)
    sbuf[ahead(1)] = product(ahead(1)).astype(BF16)
    partial_send(ahead(1), rbuf, behind(1), 1)
    sbuf[behind(1)] = product(behind(1)).astype(BF16)
    partial_send(behind(1), rbuf, ahead(1), -1)
    proj[...] = product(ahead(3))
    text(2, 1)
    arrived(rbuf.at[7], p_recv.at[7])
    sbuf[ahead(3)] = (proj[...] + rbuf[7].astype(F32)).astype(BF16)
    partial_send(ahead(3), rbuf, behind(3), 3)
    proj[...] = product(behind(2))
    arrived(rbuf.at[0], p_recv.at[0])
    sbuf[behind(2)] = (proj[...] + rbuf[0].astype(F32)).astype(BF16)
    partial_send(behind(2), rbuf, ahead(2), -2)
    proj[...] = product(0)
    text(3, 3)

    def square_step(j, square):
        arrived(sumsq_in.at[j], q_recv.at[j])
        return square + sumsq_in[j]

    square = lax.fori_loop(1, 8, square_step, sumsq[...])
    inv = lax.rsqrt(square * (1.0 / 8192.0) + 1e-06)
    inv = jnp.broadcast_to(inv[:1], (HALF, HALF)).T
    for slot in (ahead(1), behind(1), behind(2), ahead(2), behind(3)):
        arrived(rbuf.at[slot], p_recv.at[slot])
        proj[...] += rbuf[slot].astype(F32)
    key = proj[:, :HEAD_DIM] * inv + kvbias_ref[:, :HEAD_DIM]
    value = proj[:, HEAD_DIM:] * inv + kvbias_ref[:, HEAD_DIM:]
    key = key * cos_ref[...] + pltpu.roll(key, HEAD_DIM // 2, 1) * sin_ref[...]
    res[:, :HEAD_DIM] = key.astype(BF16)
    res[:, HEAD_DIM:] = value.astype(BF16)
    send(res, res_in, o_sem.at[0], o_sem.at[1], partner)
    out_ref[mine, :] = res[...]
    text(6, 2)
    arrived(res_in, o_sem.at[1])
    out_ref[theirs, :] = res_in[...]
    for copy in started:
        copy.wait_send()

    def sent_step(j, carry):
        sumsq_copy(j).wait_send()
        return carry

    lax.fori_loop(1, 8, sent_step, 0)


def gather_project(vis, w, kvw, mbias, gain, kvbias, pos, q, tkv):
    rollouts = q.shape[0] // RLEN
    heads = q.shape[1] // HEAD_DIM
    vmem = pl.BlockSpec(memory_space=pltpu.VMEM)
    hbm = pl.BlockSpec(memory_space=pltpu.HBM)
    dma = pltpu.SemaphoreType.DMA
    return pl.pallas_call(
        gather_project_kernel,
        out_shape=(
            pltpu.VMEM((ROWS, 2 * HEAD_DIM), BF16),
            pltpu.VMEM((rollouts, heads * RLEN, 2 * HEAD_DIM), F32),
            pltpu.VMEM((rollouts, heads * RLEN, HEAD_DIM), F32),
        ),
        in_specs=[hbm] * 9,
        out_specs=(vmem, vmem, vmem),
        scratch_shapes=[
            pltpu.VMEM((1, COLS), F32),
            pltpu.VMEM((1, 8192), F32),
            pltpu.VMEM((1, 2 * HEAD_DIM), F32),
            pltpu.VMEM((3, ROWS), jnp.int32),
            pltpu.VMEM((HALF, HEAD_DIM), F32),
            pltpu.VMEM((HALF, HEAD_DIM), F32),
            pltpu.VMEM(q.shape, BF16),
            pltpu.VMEM(tkv.shape, BF16),
            pltpu.VMEM((ROWS, 5120), BF16),
            pltpu.VMEM((8, ROWS, PAIR), BF16),
            pltpu.VMEM((8, PAIR, COLS), BF16),
            pltpu.VMEM((8, 1024, 2 * HEAD_DIM), BF16),
            pltpu.VMEM((ROWS, COLS), F32),
            pltpu.VMEM((ROWS, COLS), BF16),
            pltpu.VMEM((2, HALF, COLS), BF16),
            pltpu.VMEM((2, HALF, COLS), BF16),
            pltpu.VMEM((8, HALF), F32),
            pltpu.VMEM((8, 8, HALF), F32),
            pltpu.VMEM((8, HALF, 2 * HEAD_DIM), BF16),
            pltpu.VMEM((8, HALF, 2 * HEAD_DIM), BF16),
            pltpu.VMEM((HALF, 2 * HEAD_DIM), F32),
            pltpu.VMEM((HALF, 2 * HEAD_DIM), BF16),
            pltpu.VMEM((HALF, 2 * HEAD_DIM), BF16),
            dma((9,)),
            dma((32,)),
            dma((32,)),
            dma((8,)),
            dma((8,)),
            dma((19,)),
            dma((19,)),
            dma((2,)),
            dma((8,)),
            dma((8,)),
            dma((8,)),
            dma((8,)),
            dma((2,)),
        ],
        compiler_params=pltpu.CompilerParams(
            collective_id=0, has_side_effects=True, vmem_limit_bytes=46 * 2**20
        ),
        cost_estimate=pl.CostEstimate(
            flops=2_500_000_000, bytes_accessed=8_000_000, transcendentals=1_500_000
        ),
        name="gather_project",
    )(vis, w, kvw, mbias, gain, kvbias, pos, q, tkv)


def attention_kernel(
    count_ref,
    length_ref,
    q_in,
    kv_in,
    text_sums,
    text_max,
    out_hbm,
    out,
    keys,
    values,
    out_sem,
):
    rollouts = length_ref.shape[0]
    live = lax.broadcasted_iota(jnp.int32, (ROWS, HEAD_DIM), 0) < count_ref[0]
    image_keys = kv_in[:, :HEAD_DIM]
    keys[...] = jnp.where(live, image_keys, image_keys[:1])
    values[:, :HEAD_DIM] = jnp.where(live, kv_in[:, HEAD_DIM:], 0.0).astype(BF16)
    values[:, HEAD_DIM:] = jnp.where(live, 1.0, 0.0).astype(BF16)
    token = lax.rem(lax.broadcasted_iota(jnp.int32, (8 * RLEN, RLEN), 0), RLEN)
    heads = [slice(h * HEAD_DIM, (h + 1) * HEAD_DIM) for h in range(8)]

    def one(r):
        rows = pl.ds(pl.multiple_of(r * RLEN, RLEN), RLEN)
        kept = token < length_ref[r]
        q = jnp.concatenate([q_in[rows, cols] for cols in heads], axis=0)
        scores = lax.dot_general(
            q, keys[...], (((1,), (1,)), ((), ())), preferred_element_type=F32
        )
        first, second = scores[:, :HEAD_DIM], scores[:, HEAD_DIM:]
        text_highest = text_max[r]
        highest = jnp.max(jnp.maximum(first, second), axis=1, keepdims=True)
        highest = jnp.maximum(highest, text_highest)
        first = jnp.exp2((first - highest) * SCORE_FACTOR)
        second = jnp.exp2((second - highest) * SCORE_FACTOR)
        scale = jnp.exp2((text_highest - highest) * SCORE_FACTOR)
        weights = jnp.concatenate([first, second], axis=1).astype(BF16)
        sums = jnp.dot(weights, values[...], preferred_element_type=F32)
        top = sums[:, :HEAD_DIM] + text_sums[r, :, :HEAD_DIM] * scale
        bottom = sums[:, HEAD_DIM:] + text_sums[r, :, HEAD_DIM:] * scale
        attended = jnp.where(kept, top / bottom, 0.0).astype(BF16)
        for i, cols in enumerate(heads):
            out[r, :, cols] = attended[i * RLEN : (i + 1) * RLEN]

    def store(r):
        rows = pl.ds(pl.multiple_of(r * RLEN, RLEN), RLEN)
        return pltpu.make_async_copy(out.at[r], out_hbm.at[rows], out_sem.at[r])

    def step(i, carry):
        for u in range(UNROLL):
            one(i * UNROLL + u)
        for u in range(UNROLL):
            store(i * UNROLL + u).start()
        return carry

    lax.fori_loop(0, rollouts // UNROLL, step, 0)

    def stored(r, carry):
        store(r).wait()
        return carry

    lax.fori_loop(0, rollouts, stored, 0)


def attention(count, length, q, kv, text_sums, text_max):
    rollouts = length.shape[0]
    smem = pl.BlockSpec(memory_space=pltpu.SMEM)
    vmem = pl.BlockSpec(memory_space=pltpu.VMEM)
    return pl.pallas_call(
        attention_kernel,
        in_specs=[smem, smem, vmem, vmem, vmem, vmem],
        out_specs=pl.BlockSpec(memory_space=pl.ANY),
        out_shape=jax.ShapeDtypeStruct(q.shape, BF16),
        scratch_shapes=[
            pltpu.VMEM((rollouts, RLEN, q.shape[1]), BF16),
            pltpu.VMEM((ROWS, HEAD_DIM), BF16),
            pltpu.VMEM((ROWS, 2 * HEAD_DIM), BF16),
            pltpu.SemaphoreType.DMA((rollouts,)),
        ],
        compiler_params=pltpu.CompilerParams(vmem_limit_bytes=24 * 2**20),
        name="attention",
    )(count, length, q, kv, text_sums, text_max)


def body(
    vis_hidden,
    merge_weight,
    merge_bias,
    norm_gain,
    kv_weight,
    kv_bias,
    queries,
    text_kv,
    image_count,
    image_pos,
    resp_length,
):
    kv, text_sums, text_max = gather_project(
        vis_hidden,
        merge_weight,
        kv_weight,
        merge_bias.reshape(1, -1),
        norm_gain.reshape(1, -1),
        kv_bias.reshape(1, -1),
        image_pos,
        queries,
        text_kv,
    )
    return attention(image_count, resp_length, queries, kv, text_sums, text_max)


def solution(mesh):
    in_specs = (
        P("group", None),
        P("group", ("roll", "tp")),
        P(("roll", "tp")),
        P(),
        P(None, "tp"),
        P("tp"),
        P(("group", "roll"), "tp"),
        P(("group", "roll"), "tp"),
        P("group"),
        P(None, "group"),
        P(("group", "roll")),
    )
    out_specs = P(("group", "roll"), "tp")
    return jax.shard_map(body, mesh=mesh, in_specs=in_specs, out_specs=out_specs, check_vma=False)
```

```python
import math

import jax
import jax.numpy as jnp
from jax import lax
from jax.experimental import pallas as pl
from jax.experimental.pallas import tpu as pltpu
from jax.sharding import PartitionSpec as P

HEAD_DIM = 128
RLEN = 128
SCORE_FACTOR = HEAD_DIM ** (-0.5) * math.log2(math.e)
UNROLL = 8
MESH = pl.DeviceIdType.MESH
BF16 = jnp.bfloat16
F32 = jnp.float32

ZOFF = (0, 1, -1, 2, -2, 3, -3, 4)
ZBACK = (0, 2, 1, 4, 3, 6, 5, 7)
KVGROUPS = ((0, 3), (3, 2), (5, 2))
FAR_SLOT = 7
SLOTS = [(0, 0), (0, 1), (0, -1), (1, 0), (0, 2), (1, 1), (1, -1), (1, 2)]
NEXT_UP, NEXT_DOWN, CROSS, FAR, CROSS_UP, CROSS_DOWN, CROSS_FAR = range(1, 8)
ROWS = 256
HALF = 128
HID = 320
PAIR = 640
COLS = 512


def gather_project_kernel(
    vis_hbm,
    w_hbm,
    kvw_hbm,
    mbias_hbm,
    gain_hbm,
    kvbias_hbm,
    pos_hbm,
    q_hbm,
    tkv_hbm,
    out_ref,
    text_sums,
    text_max,
    mbias_ref,
    gain_ref,
    kvbias_ref,
    pos_ref,
    cos_ref,
    sin_ref,
    q_in,
    tkv_in,
    vis,
    act,
    wbuf,
    kvbuf,
    acc,
    visual,
    xs,
    xg,
    sumsq,
    sumsq_in,
    sbuf,
    rbuf,
    proj,
    res,
    res_in,
    local_sem,
    w_send,
    w_recv,
    kz_send,
    kz_recv,
    kx_send,
    kx_recv,
    v_sem,
    q_send,
    q_recv,
    p_send,
    p_recv,
    o_sem,
):
    g = lax.axis_index("group")
    roll = lax.axis_index("roll")
    z = lax.axis_index("tp")
    hi = g // 8
    y = lax.rem(g // 2, 4)
    core = lax.rem(g, 2)
    x = 2 * hi + roll
    me_k = hi * 4 + y

    def at(dx=0, dy=0, dz=0, sib=False):
        xx = lax.rem(x + dx + 4, 4)
        yy = lax.rem(y + dy + 4, 4)
        zz = lax.rem(z + dz + 8, 8)
        cc = 1 - core if sib else core
        return ((xx // 2) * 8 + yy * 2 + cc, lax.rem(xx, 2), zz)

    def k_of(dh, dy):
        hh = 1 - hi if dh else hi
        return hh * 4 + lax.rem(y + dy + 4, 4)

    started = []

    def send(src, dst, ssem, rsem, device):
        copy = pltpu.make_async_remote_copy(
            src_ref=src,
            dst_ref=dst,
            send_sem=ssem,
            recv_sem=rsem,
            device_id=device,
            device_id_type=MESH,
        )
        copy.start()
        started.append(copy)

    def arrived(dst, rsem):
        pltpu.make_async_remote_copy(
            src_ref=dst,
            dst_ref=dst,
            send_sem=rsem,
            recv_sem=rsem,
            device_id=at(sib=True),
            device_id_type=MESH,
        ).wait_recv()

    part_start = roll * COLS + core * ROWS

    def kv_piece(first, count, start, rows):
        return kvbuf.at[pl.ds(first, count), pl.ds(pl.multiple_of(start, HALF), rows)]

    def kv_rows(zz):
        start = roll * 4096 + zz * COLS + core * ROWS
        return pl.ds(pl.multiple_of(start, ROWS), ROWS)

    quarter = x * 2 + core

    def far_rows(zz):
        start = (quarter // 4) * 4096 + zz * COLS + lax.rem(quarter, 4) * HALF
        return pl.ds(pl.multiple_of(start, HALF), HALF)

    def far_piece(part):
        return kvbuf.at[FAR_SLOT, pl.ds(pl.multiple_of(part * HALF, HALF), HALF)]

    def kv_slot(j):
        return kvbuf.at[j, pl.ds(pl.multiple_of(part_start, ROWS), ROWS)]

    def w_piece(slot, half, cc):
        dh, dy = SLOTS[slot]
        start, rows = (0, HID) if half is None else (half * (HID // 2), HID // 2)
        return wbuf.at[k_of(dh, dy), pl.ds(pl.multiple_of(cc * HID + start, 32), rows)]

    own_w = pltpu.make_async_copy(w_hbm, w_piece(0, None, core), local_sem.at[0])
    own_kv = pltpu.make_async_copy(kvw_hbm.at[kv_rows(z)], kv_slot(0), local_sem.at[1])
    own_vis = pltpu.make_async_copy(vis_hbm, vis, local_sem.at[2])
    own_w.start()
    own_kv.start()
    own_vis.start()
    small = [
        pltpu.make_async_copy(src, dst, local_sem.at[3 + i])
        for i, (src, dst) in enumerate(
            (
                (mbias_hbm, mbias_ref),
                (gain_hbm, gain_ref),
                (kvbias_hbm, kvbias_ref),
                (pos_hbm, pos_ref),
                (tkv_hbm, tkv_in),
                (q_hbm, q_in),
            )
        )
    ]
    for copy in small:
        copy.start()

    partners = [at(dx=1), at(dx=-1), at(dx=2), at(dy=1), at(dy=-1), at(dy=2), at(sib=True)]
    partners += [at(dz=d) for d in ZOFF[1:]]
    barrier = pltpu.get_barrier_semaphore()
    for partner in partners:
        pl.semaphore_signal(barrier, inc=1, device_id=partner, device_id_type=MESH)
    pl.semaphore_wait(barrier, len(partners))

    sent = iter(range(64))
    kx_sent = iter(range(64))

    def w_send_to(slot, half, dx=0, dy=0):
        dh, ddy = SLOTS[slot]
        there = SLOTS.index(((dh + (1 if dx else 0)) % 2, (ddy - dy + 1) % 4 - 1))
        block = w_piece(slot, half, core)
        send(block, block, w_send.at[next(sent)], w_recv.at[there * 2 + half], at(dx=dx, dy=dy))

    def w_wait(slot, half):
        arrived(w_piece(slot, half, core), w_recv.at[slot * 2 + half])

    def w_sibling(slot, half=None):
        block = w_piece(slot, half, core)
        index = 16 + slot * 2 + (half or 0)
        send(block, block, w_send.at[next(sent)], w_recv.at[index], at(sib=True))

    def w_sibling_wait(slot, half=None):
        arrived(w_piece(slot, half, 1 - core), w_recv.at[16 + slot * 2 + (half or 0)])

    own_w.wait()
    for half in (0, 1):
        w_send_to(0, half, dx=2)
    send(
        kvw_hbm.at[far_rows(lax.rem(z + 4, 8))],
        far_piece(quarter),
        kz_send.at[FAR_SLOT],
        kz_recv.at[FAR_SLOT],
        at(dz=4),
    )
    for j in (1, 2, 3, 4, 5, 6):
        zz = lax.rem(z + ZOFF[j] + 8, 8)
        send(
            kvw_hbm.at[kv_rows(zz)],
            kv_slot(ZBACK[j]),
            kz_send.at[j],
            kz_recv.at[ZBACK[j]],
            at(dz=ZOFF[j]),
        )
    for half in (0, 1):
        w_send_to(0, half, dy=1)
        w_send_to(0, 1 - half, dy=-1)

    own_vis.wait()

    def activate(k):
        def step(i, carry):
            rows = pl.ds(pl.multiple_of(i * 32, 32), 32)
            v = vis[rows, k * PAIR : (k + 1) * PAIR].astype(F32)
            act[k, rows] = (v * (1.0 + lax.erf(v * (1.0 / math.sqrt(2.0)))) * 0.5).astype(BF16)
            return carry

        lax.fori_loop(0, ROWS // 32, step, 0)

    def merge(count, chip):
        def step(i, carry):
            k = chip(i)
            acc[...] += jnp.dot(act[k], wbuf[k], preferred_element_type=F32)
            return carry

        lax.fori_loop(0, count, step, 0)

    def kv_share(group):
        first, count = KVGROUPS[group]
        for j in range(first, first + count):
            if j:
                arrived(kv_slot(j), kz_recv.at[j])
        for i, dx in ((0, 1), (1, -1)):
            block = kv_piece(first, count, part_start + i * HALF, HALF)
            send(block, block, kx_send.at[next(kx_sent)], kx_recv.at[group * 4 + i], at(dx=dx))
        block = kv_piece(first, count, part_start, ROWS)
        send(block, block, kx_send.at[next(kx_sent)], kx_recv.at[group * 4 + 2], at(sib=True))

    other_start = (1 - roll) * COLS + core * ROWS

    def kv_pass(group):
        first, count = KVGROUPS[group]
        for i in (0, 1):
            block = kv_piece(first, count, other_start + i * HALF, HALF)
            arrived(block, kx_recv.at[group * 4 + i])
        block = kv_piece(first, count, other_start, ROWS)
        send(block, block, kx_send.at[next(kx_sent)], kx_recv.at[group * 4 + 3], at(sib=True))

    far_sources = ((1, 13), (-1, 14), (2, 15))

    def far_at(dx, cc):
        return far_piece(lax.rem(x + dx + 4, 4) * 2 + cc)

    def far_share():
        block = far_piece(quarter)
        arrived(block, kz_recv.at[FAR_SLOT])
        for dx, index in ((2, 15), (1, 14), (-1, 13)):
            send(block, block, kx_send.at[next(kx_sent)], kx_recv.at[index], at(dx=dx))
        send(block, block, kx_send.at[next(kx_sent)], kx_recv.at[12], at(sib=True))

    def far_pass():
        for dx, index in far_sources:
            block = far_at(dx, core)
            arrived(block, kx_recv.at[index])
            send(block, block, kx_send.at[next(kx_sent)], kx_recv.at[index + 3], at(sib=True))

    def far_end():
        arrived(far_at(0, 1 - core), kx_recv.at[12])
        for dx, index in far_sources:
            arrived(far_at(dx, 1 - core), kx_recv.at[index + 3])

    def kv_end(group):
        first, count = KVGROUPS[group]
        for i, rr in ((2, roll), (3, 1 - roll)):
            block = kv_piece(first, count, rr * COLS + (1 - core) * ROWS, ROWS)
            arrived(block, kx_recv.at[group * 4 + i])

    token = lax.rem(lax.broadcasted_iota(jnp.int32, (8 * RLEN, RLEN), 0), RLEN)
    causal = lax.broadcasted_iota(jnp.int32, (8 * RLEN, RLEN), 1) <= token

    def text(first, count):
        def step(r, carry):
            rows = pl.ds(pl.multiple_of(r * RLEN, RLEN), RLEN)
            q = jnp.concatenate(
                [q_in[rows, h * HEAD_DIM : (h + 1) * HEAD_DIM] for h in range(8)], axis=0
            )
            scores = lax.dot_general(
                q,
                tkv_in[rows, :HEAD_DIM],
                (((1,), (1,)), ((), ())),
                preferred_element_type=F32,
            )
            scores = jnp.where(causal, scores, -1e30)
            highest = jnp.max(scores, axis=1, keepdims=True)
            weights = jnp.exp2((scores - highest) * SCORE_FACTOR).astype(BF16)
            values = jnp.concatenate(
                [tkv_in[rows, HEAD_DIM:], jnp.ones((RLEN, HEAD_DIM), BF16)], axis=1
            )
            text_sums[r] = jnp.dot(weights, values, preferred_element_type=F32)
            text_max[r] = jnp.broadcast_to(highest, (8 * RLEN, HEAD_DIM))
            return carry

        lax.fori_loop(first, first + count, step, 0)

    activate(0)
    activate(1)
    for copy in small:
        copy.wait()
    w_wait(NEXT_DOWN, 0)
    w_send_to(NEXT_DOWN, 0, dy=1)
    w_wait(NEXT_UP, 1)
    w_send_to(NEXT_UP, 1, dy=-1)
    activate(2)
    for half in (0, 1):
        w_wait(CROSS, half)
        w_send_to(CROSS, half, dy=1)
        w_send_to(CROSS, half, dy=-1)
        activate(3 + half)
    own_kv.wait()
    kv_share(0)
    w_sibling(0)
    w_sibling(CROSS)
    w_wait(NEXT_DOWN, 1)
    w_sibling(NEXT_DOWN)
    w_wait(NEXT_UP, 0)
    w_sibling(NEXT_UP)
    activate(5)
    kv_share(1)
    far_share()
    kv_pass(0)
    w_wait(CROSS_DOWN, 0)
    w_send_to(CROSS_DOWN, 0, dy=1)
    w_wait(CROSS_UP, 1)
    w_send_to(CROSS_UP, 1, dy=-1)
    activate(6)
    for half in (0, 1):
        w_wait(FAR, half)
    w_sibling(FAR)
    kv_share(2)
    activate(7)
    mine = pl.ds(pl.multiple_of(roll * HALF, HALF), HALF)
    theirs = pl.ds(pl.multiple_of((1 - roll) * HALF, HALF), HALF)
    lane = lax.broadcasted_iota(jnp.int32, (HALF, HEAD_DIM), 1)
    freq = lax.rem(lane, HEAD_DIM // 2)
    pos = pos_ref[:, mine].astype(F32)
    by_row = [jnp.broadcast_to(pos[s : s + 1], (HALF, HEAD_DIM)).T for s in range(3)]
    chosen = jnp.where(freq < 16, by_row[0], jnp.where(freq < 40, by_row[1], by_row[2]))
    angle = chosen * jnp.exp(freq.astype(F32) * (-2.0 * math.log(1e6) / HEAD_DIM))
    sine = jnp.sin(angle)
    cos_ref[...] = jnp.cos(angle)
    sin_ref[...] = jnp.where(lane < HEAD_DIM // 2, -sine, sine)

    acc[...] = jnp.broadcast_to(mbias_ref[...], acc.shape)
    w_wait(CROSS_DOWN, 1)
    w_sibling(CROSS_DOWN)
    w_wait(CROSS_UP, 0)
    w_sibling(CROSS_UP)
    for slot in (0, NEXT_DOWN, NEXT_UP, FAR):
        w_sibling_wait(slot)
    merge(4, lambda i: hi * 4 + i)
    for half in (0, 1):
        w_wait(CROSS_FAR, half)
        w_sibling(CROSS_FAR, half)
    kv_pass(1)
    for slot in (CROSS, CROSS_DOWN, CROSS_UP):
        w_sibling_wait(slot)
    merge(3, lambda i: (1 - hi) * 4 + lax.rem(y + i + 3, 4))
    for half in (0, 1):
        w_sibling_wait(CROSS_FAR, half)
    merge(1, lambda i: (1 - hi) * 4 + lax.rem(y + 2, 4))

    visual[...] = acc[...].astype(BF16)
    partner = (g, 1 - roll, z)
    send(visual.at[theirs], xs.at[roll], v_sem.at[0], v_sem.at[1], partner)
    kv_pass(2)
    far_pass()
    xs[roll] = visual[mine, :]
    text(0, 2)
    for group in range(3):
        kv_end(group)
    far_end()
    arrived(xs.at[1 - roll], v_sem.at[1])

    def feature_start(r):
        return pl.multiple_of(r * 4096 + z * COLS, COLS)

    for r in range(2):
        xg[r] = (xs[r].astype(F32) * gain_ref[:, pl.ds(feature_start(r), COLS)]).astype(BF16)

    def product(j):
        return jnp.dot(xg[0], kvbuf[j, :COLS], preferred_element_type=F32) + jnp.dot(
            xg[1], kvbuf[j, COLS:], preferred_element_type=F32
        )

    def sumsq_copy(j):
        sign = 2 * lax.rem(j, 2) - 1
        back = j + sign * (1 - j // 7)
        return pltpu.make_async_remote_copy(
            src_ref=sumsq,
            dst_ref=sumsq_in.at[back],
            send_sem=q_send.at[j],
            recv_sem=q_recv.at[back],
            device_id=at(dz=(j + 1) // 2 * sign),
            device_id_type=MESH,
        )

    def sumsq_send(i, carry):
        sumsq_copy(i).start()
        return carry

    way = 1 - 2 * core

    def ahead(k):
        return 2 * k - 1 + core

    def behind(k):
        return 2 * k - core

    def partial_send(j, dst, slot, steps):
        send(sbuf.at[j], dst.at[slot], p_send.at[j], p_recv.at[slot], at(dz=way * steps))

    total = jnp.zeros((HALF, 1), F32)
    for r in range(2):
        v = xs[r].astype(F32)
        total += jnp.sum(v * v, axis=1, keepdims=True)
    sumsq[...] = jnp.broadcast_to(total, (HALF, HALF)).T[:8]
    lax.fori_loop(1, 8, sumsq_send, 0)
    proj[...] = product(ahead(3))
    sbuf[7] = product(7).astype(BF16)
    partial_send(7, rbuf, 7, 1)
    sbuf[behind(3)] = product(behind(3)).astype(BF16)
    partial_send(behind(3), rbuf, 0, -1)
    sbuf[ahead(2)] = product(ahead(2)).astype(BF16)
    partial_send(ahead(2), rbuf, behind(2), 2)
    sbuf[ahead(1)] = product(ahead(1)).astype(BF16)
    partial_send(ahead(1), rbuf, behind(1), 1)
    sbuf[behind(1)] = product(behind(1)).astype(BF16)
    partial_send(behind(1), rbuf, ahead(1), -1)
    arrived(rbuf.at[7], p_recv.at[7])
    sbuf[ahead(3)] = (proj[...] + rbuf[7].astype(F32)).astype(BF16)
    partial_send(ahead(3), rbuf, behind(3), 3)
    proj[...] = product(behind(2))
    arrived(rbuf.at[0], p_recv.at[0])
    sbuf[behind(2)] = (proj[...] + rbuf[0].astype(F32)).astype(BF16)
    partial_send(behind(2), rbuf, ahead(2), -2)
    proj[...] = product(0)
    text(2, 4)
    for copy in started:
        copy.wait_send()
    started.clear()

    def square_step(j, square):
        arrived(sumsq_in.at[j], q_recv.at[j])
        return square + sumsq_in[j]

    square = lax.fori_loop(1, 8, square_step, sumsq[...])
    inv = lax.rsqrt(square * (1.0 / 8192.0) + 1e-06)
    inv = jnp.broadcast_to(inv[:1], (HALF, HALF)).T
    for slot in (ahead(1), behind(1), behind(2), ahead(2), behind(3)):
        arrived(rbuf.at[slot], p_recv.at[slot])
        proj[...] += rbuf[slot].astype(F32)
    key = proj[:, :HEAD_DIM] * inv + kvbias_ref[:, :HEAD_DIM]
    value = proj[:, HEAD_DIM:] * inv + kvbias_ref[:, HEAD_DIM:]
    key = key * cos_ref[...] + pltpu.roll(key, HEAD_DIM // 2, 1) * sin_ref[...]
    res[:, :HEAD_DIM] = key.astype(BF16)
    res[:, HEAD_DIM:] = value.astype(BF16)
    send(res, res_in, o_sem.at[0], o_sem.at[1], partner)
    out_ref[mine, :] = res[...]
    text(6, 2)
    arrived(res_in, o_sem.at[1])
    out_ref[theirs, :] = res_in[...]
    for copy in started:
        copy.wait_send()

    def sent_step(j, carry):
        sumsq_copy(j).wait_send()
        return carry

    lax.fori_loop(1, 8, sent_step, 0)


def gather_project(vis, w, kvw, mbias, gain, kvbias, pos, q, tkv):
    rollouts = q.shape[0] // RLEN
    heads = q.shape[1] // HEAD_DIM
    vmem = pl.BlockSpec(memory_space=pltpu.VMEM)
    hbm = pl.BlockSpec(memory_space=pltpu.HBM)
    dma = pltpu.SemaphoreType.DMA
    return pl.pallas_call(
        gather_project_kernel,
        out_shape=(
            pltpu.VMEM((ROWS, 2 * HEAD_DIM), BF16),
            pltpu.VMEM((rollouts, heads * RLEN, 2 * HEAD_DIM), F32),
            pltpu.VMEM((rollouts, heads * RLEN, HEAD_DIM), F32),
        ),
        in_specs=[hbm] * 9,
        out_specs=(vmem, vmem, vmem),
        scratch_shapes=[
            pltpu.VMEM((1, COLS), F32),
            pltpu.VMEM((1, 8192), F32),
            pltpu.VMEM((1, 2 * HEAD_DIM), F32),
            pltpu.VMEM((3, ROWS), jnp.int32),
            pltpu.VMEM((HALF, HEAD_DIM), F32),
            pltpu.VMEM((HALF, HEAD_DIM), F32),
            pltpu.VMEM(q.shape, BF16),
            pltpu.VMEM(tkv.shape, BF16),
            pltpu.VMEM((ROWS, 5120), BF16),
            pltpu.VMEM((8, ROWS, PAIR), BF16),
            pltpu.VMEM((8, PAIR, COLS), BF16),
            pltpu.VMEM((8, 1024, 2 * HEAD_DIM), BF16),
            pltpu.VMEM((ROWS, COLS), F32),
            pltpu.VMEM((ROWS, COLS), BF16),
            pltpu.VMEM((2, HALF, COLS), BF16),
            pltpu.VMEM((2, HALF, COLS), BF16),
            pltpu.VMEM((8, HALF), F32),
            pltpu.VMEM((8, 8, HALF), F32),
            pltpu.VMEM((8, HALF, 2 * HEAD_DIM), BF16),
            pltpu.VMEM((8, HALF, 2 * HEAD_DIM), BF16),
            pltpu.VMEM((HALF, 2 * HEAD_DIM), F32),
            pltpu.VMEM((HALF, 2 * HEAD_DIM), BF16),
            pltpu.VMEM((HALF, 2 * HEAD_DIM), BF16),
            dma((9,)),
            dma((32,)),
            dma((32,)),
            dma((8,)),
            dma((8,)),
            dma((19,)),
            dma((19,)),
            dma((2,)),
            dma((8,)),
            dma((8,)),
            dma((8,)),
            dma((8,)),
            dma((2,)),
        ],
        compiler_params=pltpu.CompilerParams(
            collective_id=0, has_side_effects=True, vmem_limit_bytes=46 * 2**20
        ),
        cost_estimate=pl.CostEstimate(
            flops=2_500_000_000, bytes_accessed=8_000_000, transcendentals=1_500_000
        ),
        name="gather_project",
    )(vis, w, kvw, mbias, gain, kvbias, pos, q, tkv)


def attention_kernel(
    count_ref,
    length_ref,
    q_in,
    kv_in,
    text_sums,
    text_max,
    out_hbm,
    out,
    keys,
    values,
    out_sem,
):
    rollouts = length_ref.shape[0]
    live = lax.broadcasted_iota(jnp.int32, (ROWS, HEAD_DIM), 0) < count_ref[0]
    image_keys = kv_in[:, :HEAD_DIM]
    keys[...] = jnp.where(live, image_keys, image_keys[:1])
    values[:, :HEAD_DIM] = jnp.where(live, kv_in[:, HEAD_DIM:], 0.0).astype(BF16)
    values[:, HEAD_DIM:] = jnp.where(live, 1.0, 0.0).astype(BF16)
    token = lax.rem(lax.broadcasted_iota(jnp.int32, (8 * RLEN, RLEN), 0), RLEN)
    heads = [slice(h * HEAD_DIM, (h + 1) * HEAD_DIM) for h in range(8)]

    def one(r):
        rows = pl.ds(pl.multiple_of(r * RLEN, RLEN), RLEN)
        kept = token < length_ref[r]
        q = jnp.concatenate([q_in[rows, cols] for cols in heads], axis=0)
        scores = lax.dot_general(
            q, keys[...], (((1,), (1,)), ((), ())), preferred_element_type=F32
        )
        first, second = scores[:, :HEAD_DIM], scores[:, HEAD_DIM:]
        text_highest = text_max[r]
        highest = jnp.max(jnp.maximum(first, second), axis=1, keepdims=True)
        highest = jnp.maximum(highest, text_highest)
        first = jnp.exp2((first - highest) * SCORE_FACTOR)
        second = jnp.exp2((second - highest) * SCORE_FACTOR)
        scale = jnp.exp2((text_highest - highest) * SCORE_FACTOR)
        weights = jnp.concatenate([first, second], axis=1).astype(BF16)
        sums = jnp.dot(weights, values[...], preferred_element_type=F32)
        top = sums[:, :HEAD_DIM] + text_sums[r, :, :HEAD_DIM] * scale
        bottom = sums[:, HEAD_DIM:] + text_sums[r, :, HEAD_DIM:] * scale
        attended = jnp.where(kept, top / bottom, 0.0).astype(BF16)
        for i, cols in enumerate(heads):
            out[r, :, cols] = attended[i * RLEN : (i + 1) * RLEN]

    def store(r):
        rows = pl.ds(pl.multiple_of(r * RLEN, RLEN), RLEN)
        return pltpu.make_async_copy(out.at[r], out_hbm.at[rows], out_sem.at[r])

    def step(i, carry):
        for u in range(UNROLL):
            one(i * UNROLL + u)
            store(i * UNROLL + u).start()
        return carry

    lax.fori_loop(0, rollouts // UNROLL, step, 0)

    def stored(r, carry):
        store(r).wait()
        return carry

    lax.fori_loop(0, rollouts, stored, 0)


def attention(count, length, q, kv, text_sums, text_max):
    rollouts = length.shape[0]
    smem = pl.BlockSpec(memory_space=pltpu.SMEM)
    vmem = pl.BlockSpec(memory_space=pltpu.VMEM)
    return pl.pallas_call(
        attention_kernel,
        in_specs=[smem, smem, vmem, vmem, vmem, vmem],
        out_specs=pl.BlockSpec(memory_space=pl.ANY),
        out_shape=jax.ShapeDtypeStruct(q.shape, BF16),
        scratch_shapes=[
            pltpu.VMEM((rollouts, RLEN, q.shape[1]), BF16),
            pltpu.VMEM((ROWS, HEAD_DIM), BF16),
            pltpu.VMEM((ROWS, 2 * HEAD_DIM), BF16),
            pltpu.SemaphoreType.DMA((rollouts,)),
        ],
        compiler_params=pltpu.CompilerParams(vmem_limit_bytes=24 * 2**20),
        name="attention",
    )(count, length, q, kv, text_sums, text_max)


def body(
    vis_hidden,
    merge_weight,
    merge_bias,
    norm_gain,
    kv_weight,
    kv_bias,
    queries,
    text_kv,
    image_count,
    image_pos,
    resp_length,
):
    kv, text_sums, text_max = gather_project(
        vis_hidden,
        merge_weight,
        kv_weight,
        merge_bias.reshape(1, -1),
        norm_gain.reshape(1, -1),
        kv_bias.reshape(1, -1),
        image_pos,
        queries,
        text_kv,
    )
    return attention(image_count, resp_length, queries, kv, text_sums, text_max)


def solution(mesh):
    in_specs = (
        P("group", None),
        P("group", ("roll", "tp")),
        P(("roll", "tp")),
        P(),
        P(None, "tp"),
        P("tp"),
        P(("group", "roll"), "tp"),
        P(("group", "roll"), "tp"),
        P("group"),
        P(None, "group"),
        P(("group", "roll")),
    )
    out_specs = P(("group", "roll"), "tp")
    return jax.shard_map(body, mesh=mesh, in_specs=in_specs, out_specs=out_specs, check_vma=False)
```

```python
import math

import jax
import jax.numpy as jnp
from jax import lax
from jax.experimental import pallas as pl
from jax.experimental.pallas import tpu as pltpu
from jax.sharding import PartitionSpec as P

HEAD_DIM = 128
RLEN = 128
SCORE_FACTOR = HEAD_DIM ** (-0.5) * math.log2(math.e)
UNROLL = 8
MESH = pl.DeviceIdType.MESH
BF16 = jnp.bfloat16
F32 = jnp.float32

ZOFF = (0, 1, -1, 2, -2, 3, -3, 4)
ZBACK = (0, 2, 1, 4, 3, 6, 5, 7)
KVGROUPS = ((0, 3), (3, 2), (5, 2))
FAR_SLOT = 7
SLOTS = [(0, 0), (0, 1), (0, -1), (1, 0), (0, 2), (1, 1), (1, -1), (1, 2)]
NEXT_UP, NEXT_DOWN, CROSS, FAR, CROSS_UP, CROSS_DOWN, CROSS_FAR = range(1, 8)
ROWS = 256
HALF = 128
HID = 320
PAIR = 640
COLS = 512


def gather_project_kernel(
    vis_hbm,
    w_hbm,
    kvw_hbm,
    mbias_hbm,
    gain_hbm,
    kvbias_hbm,
    pos_hbm,
    q_hbm,
    tkv_hbm,
    out_ref,
    text_sums,
    text_max,
    mbias_ref,
    gain_ref,
    kvbias_ref,
    pos_ref,
    cos_ref,
    sin_ref,
    q_in,
    tkv_in,
    vis,
    act,
    wbuf,
    kvbuf,
    acc,
    visual,
    xs,
    xg,
    sumsq,
    sumsq_in,
    sbuf,
    rbuf,
    proj,
    own_part,
    res,
    res_in,
    local_sem,
    w_send,
    w_recv,
    kz_send,
    kz_recv,
    kx_send,
    kx_recv,
    v_sem,
    q_send,
    q_recv,
    p_send,
    p_recv,
    o_sem,
):
    g = lax.axis_index("group")
    roll = lax.axis_index("roll")
    z = lax.axis_index("tp")
    hi = g // 8
    y = lax.rem(g // 2, 4)
    core = lax.rem(g, 2)
    x = 2 * hi + roll
    me_k = hi * 4 + y

    def at(dx=0, dy=0, dz=0, sib=False):
        xx = lax.rem(x + dx + 4, 4)
        yy = lax.rem(y + dy + 4, 4)
        zz = lax.rem(z + dz + 8, 8)
        cc = 1 - core if sib else core
        return ((xx // 2) * 8 + yy * 2 + cc, lax.rem(xx, 2), zz)

    def k_of(dh, dy):
        hh = 1 - hi if dh else hi
        return hh * 4 + lax.rem(y + dy + 4, 4)

    started = []

    def send(src, dst, ssem, rsem, device):
        copy = pltpu.make_async_remote_copy(
            src_ref=src,
            dst_ref=dst,
            send_sem=ssem,
            recv_sem=rsem,
            device_id=device,
            device_id_type=MESH,
        )
        copy.start()
        started.append(copy)

    def arrived(dst, rsem):
        pltpu.make_async_remote_copy(
            src_ref=dst,
            dst_ref=dst,
            send_sem=rsem,
            recv_sem=rsem,
            device_id=at(sib=True),
            device_id_type=MESH,
        ).wait_recv()

    part_start = roll * COLS + core * ROWS

    def kv_piece(first, count, start, rows):
        return kvbuf.at[pl.ds(first, count), pl.ds(pl.multiple_of(start, HALF), rows)]

    def kv_rows(zz):
        start = roll * 4096 + zz * COLS + core * ROWS
        return pl.ds(pl.multiple_of(start, ROWS), ROWS)

    quarter = x * 2 + core

    def far_rows(zz):
        start = (quarter // 4) * 4096 + zz * COLS + lax.rem(quarter, 4) * HALF
        return pl.ds(pl.multiple_of(start, HALF), HALF)

    def far_piece(part):
        return kvbuf.at[FAR_SLOT, pl.ds(pl.multiple_of(part * HALF, HALF), HALF)]

    def kv_slot(j):
        return kvbuf.at[j, pl.ds(pl.multiple_of(part_start, ROWS), ROWS)]

    def w_piece(slot, half, cc):
        dh, dy = SLOTS[slot]
        start, rows = (0, HID) if half is None else (half * (HID // 2), HID // 2)
        return wbuf.at[k_of(dh, dy), pl.ds(pl.multiple_of(cc * HID + start, 32), rows)]

    own_w = pltpu.make_async_copy(w_hbm, w_piece(0, None, core), local_sem.at[0])
    own_kv = pltpu.make_async_copy(kvw_hbm.at[kv_rows(z)], kv_slot(0), local_sem.at[1])
    own_vis = pltpu.make_async_copy(vis_hbm, vis, local_sem.at[2])
    own_w.start()
    own_kv.start()
    own_vis.start()
    small = [
        pltpu.make_async_copy(src, dst, local_sem.at[3 + i])
        for i, (src, dst) in enumerate(
            (
                (mbias_hbm, mbias_ref),
                (gain_hbm, gain_ref),
                (kvbias_hbm, kvbias_ref),
                (pos_hbm, pos_ref),
                (tkv_hbm, tkv_in),
                (q_hbm, q_in),
            )
        )
    ]
    for copy in small:
        copy.start()

    partners = [at(dx=1), at(dx=-1), at(dx=2), at(dy=1), at(dy=-1), at(dy=2), at(sib=True)]
    partners += [at(dz=d) for d in ZOFF[1:]]
    barrier = pltpu.get_barrier_semaphore()
    for partner in partners:
        pl.semaphore_signal(barrier, inc=1, device_id=partner, device_id_type=MESH)
    pl.semaphore_wait(barrier, len(partners))

    sent = iter(range(64))
    kx_sent = iter(range(64))

    def w_send_to(slot, half, dx=0, dy=0):
        dh, ddy = SLOTS[slot]
        there = SLOTS.index(((dh + (1 if dx else 0)) % 2, (ddy - dy + 1) % 4 - 1))
        block = w_piece(slot, half, core)
        send(block, block, w_send.at[next(sent)], w_recv.at[there * 2 + half], at(dx=dx, dy=dy))

    def w_wait(slot, half):
        arrived(w_piece(slot, half, core), w_recv.at[slot * 2 + half])

    def w_sibling(slot, half=None):
        block = w_piece(slot, half, core)
        index = 16 + slot * 2 + (half or 0)
        send(block, block, w_send.at[next(sent)], w_recv.at[index], at(sib=True))

    def w_sibling_wait(slot, half=None):
        arrived(w_piece(slot, half, 1 - core), w_recv.at[16 + slot * 2 + (half or 0)])

    own_w.wait()
    for half in (0, 1):
        w_send_to(0, half, dx=2)
    send(
        kvw_hbm.at[far_rows(lax.rem(z + 4, 8))],
        far_piece(quarter),
        kz_send.at[FAR_SLOT],
        kz_recv.at[FAR_SLOT],
        at(dz=4),
    )
    for j in (1, 2, 3, 4, 5, 6):
        zz = lax.rem(z + ZOFF[j] + 8, 8)
        send(
            kvw_hbm.at[kv_rows(zz)],
            kv_slot(ZBACK[j]),
            kz_send.at[j],
            kz_recv.at[ZBACK[j]],
            at(dz=ZOFF[j]),
        )
    for half in (0, 1):
        w_send_to(0, half, dy=1)
        w_send_to(0, 1 - half, dy=-1)

    own_vis.wait()

    def activate(k):
        def step(i, carry):
            rows = pl.ds(pl.multiple_of(i * 32, 32), 32)
            v = vis[rows, k * PAIR : (k + 1) * PAIR].astype(F32)
            act[k, rows] = (v * (1.0 + lax.erf(v * (1.0 / math.sqrt(2.0)))) * 0.5).astype(BF16)
            return carry

        lax.fori_loop(0, ROWS // 32, step, 0)

    def merge(count, chip):
        def step(i, carry):
            k = chip(i)
            acc[...] += jnp.dot(act[k], wbuf[k], preferred_element_type=F32)
            return carry

        lax.fori_loop(0, count, step, 0)

    def kv_share(group):
        first, count = KVGROUPS[group]
        for j in range(first, first + count):
            if j:
                arrived(kv_slot(j), kz_recv.at[j])
        for i, dx in ((0, 1), (1, -1)):
            block = kv_piece(first, count, part_start + i * HALF, HALF)
            send(block, block, kx_send.at[next(kx_sent)], kx_recv.at[group * 4 + i], at(dx=dx))
        block = kv_piece(first, count, part_start, ROWS)
        send(block, block, kx_send.at[next(kx_sent)], kx_recv.at[group * 4 + 2], at(sib=True))

    other_start = (1 - roll) * COLS + core * ROWS

    def kv_pass(group):
        first, count = KVGROUPS[group]
        for i in (0, 1):
            block = kv_piece(first, count, other_start + i * HALF, HALF)
            arrived(block, kx_recv.at[group * 4 + i])
        block = kv_piece(first, count, other_start, ROWS)
        send(block, block, kx_send.at[next(kx_sent)], kx_recv.at[group * 4 + 3], at(sib=True))

    far_sources = ((1, 13), (-1, 14), (2, 15))

    def far_at(dx, cc):
        return far_piece(lax.rem(x + dx + 4, 4) * 2 + cc)

    def far_share():
        block = far_piece(quarter)
        arrived(block, kz_recv.at[FAR_SLOT])
        for dx, index in ((2, 15), (1, 14), (-1, 13)):
            send(block, block, kx_send.at[next(kx_sent)], kx_recv.at[index], at(dx=dx))
        send(block, block, kx_send.at[next(kx_sent)], kx_recv.at[12], at(sib=True))

    def far_pass():
        for dx, index in far_sources:
            block = far_at(dx, core)
            arrived(block, kx_recv.at[index])
            send(block, block, kx_send.at[next(kx_sent)], kx_recv.at[index + 3], at(sib=True))

    def far_end():
        arrived(far_at(0, 1 - core), kx_recv.at[12])
        for dx, index in far_sources:
            arrived(far_at(dx, 1 - core), kx_recv.at[index + 3])

    def kv_end(group):
        first, count = KVGROUPS[group]
        for i, rr in ((2, roll), (3, 1 - roll)):
            block = kv_piece(first, count, rr * COLS + (1 - core) * ROWS, ROWS)
            arrived(block, kx_recv.at[group * 4 + i])

    token = lax.rem(lax.broadcasted_iota(jnp.int32, (8 * RLEN, RLEN), 0), RLEN)
    causal = lax.broadcasted_iota(jnp.int32, (8 * RLEN, RLEN), 1) <= token

    def text(first, count):
        def step(r, carry):
            rows = pl.ds(pl.multiple_of(r * RLEN, RLEN), RLEN)
            q = jnp.concatenate(
                [q_in[rows, h * HEAD_DIM : (h + 1) * HEAD_DIM] for h in range(8)], axis=0
            )
            scores = lax.dot_general(
                q,
                tkv_in[rows, :HEAD_DIM],
                (((1,), (1,)), ((), ())),
                preferred_element_type=F32,
            )
            scores = jnp.where(causal, scores, -1e30)
            highest = jnp.max(scores, axis=1, keepdims=True)
            weights = jnp.exp2((scores - highest) * SCORE_FACTOR).astype(BF16)
            values = jnp.concatenate(
                [tkv_in[rows, HEAD_DIM:], jnp.ones((RLEN, HEAD_DIM), BF16)], axis=1
            )
            text_sums[r] = jnp.dot(weights, values, preferred_element_type=F32)
            text_max[r] = jnp.broadcast_to(highest, (8 * RLEN, HEAD_DIM))
            return carry

        lax.fori_loop(first, first + count, step, 0)

    activate(0)
    activate(1)
    for copy in small:
        copy.wait()
    w_wait(NEXT_DOWN, 0)
    w_send_to(NEXT_DOWN, 0, dy=1)
    w_wait(NEXT_UP, 1)
    w_send_to(NEXT_UP, 1, dy=-1)
    activate(2)
    for half in (0, 1):
        w_wait(CROSS, half)
        w_send_to(CROSS, half, dy=1)
        w_send_to(CROSS, half, dy=-1)
        activate(3 + half)
    own_kv.wait()
    kv_share(0)
    w_sibling(0)
    w_sibling(CROSS)
    w_wait(NEXT_DOWN, 1)
    w_sibling(NEXT_DOWN)
    w_wait(NEXT_UP, 0)
    w_sibling(NEXT_UP)
    activate(5)
    kv_share(1)
    far_share()
    kv_pass(0)
    w_wait(CROSS_DOWN, 0)
    w_send_to(CROSS_DOWN, 0, dy=1)
    w_wait(CROSS_UP, 1)
    w_send_to(CROSS_UP, 1, dy=-1)
    activate(6)
    for half in (0, 1):
        w_wait(FAR, half)
    w_sibling(FAR)
    kv_share(2)
    activate(7)
    mine = pl.ds(pl.multiple_of(roll * HALF, HALF), HALF)
    theirs = pl.ds(pl.multiple_of((1 - roll) * HALF, HALF), HALF)
    lane = lax.broadcasted_iota(jnp.int32, (HALF, HEAD_DIM), 1)
    freq = lax.rem(lane, HEAD_DIM // 2)
    pos = pos_ref[:, mine].astype(F32)
    by_row = [jnp.broadcast_to(pos[s : s + 1], (HALF, HEAD_DIM)).T for s in range(3)]
    chosen = jnp.where(freq < 16, by_row[0], jnp.where(freq < 40, by_row[1], by_row[2]))
    angle = chosen * jnp.exp(freq.astype(F32) * (-2.0 * math.log(1e6) / HEAD_DIM))
    sine = jnp.sin(angle)
    cos_ref[...] = jnp.cos(angle)
    sin_ref[...] = jnp.where(lane < HEAD_DIM // 2, -sine, sine)

    acc[...] = jnp.broadcast_to(mbias_ref[...], acc.shape)
    w_wait(CROSS_DOWN, 1)
    w_sibling(CROSS_DOWN)
    w_wait(CROSS_UP, 0)
    w_sibling(CROSS_UP)
    for slot in (0, NEXT_DOWN, NEXT_UP, FAR):
        w_sibling_wait(slot)
    merge(4, lambda i: hi * 4 + i)
    for half in (0, 1):
        w_wait(CROSS_FAR, half)
        w_sibling(CROSS_FAR, half)
    kv_pass(1)
    for slot in (CROSS, CROSS_DOWN, CROSS_UP):
        w_sibling_wait(slot)
    merge(3, lambda i: (1 - hi) * 4 + lax.rem(y + i + 3, 4))
    for half in (0, 1):
        w_sibling_wait(CROSS_FAR, half)
    merge(1, lambda i: (1 - hi) * 4 + lax.rem(y + 2, 4))

    visual[...] = acc[...].astype(BF16)
    partner = (g, 1 - roll, z)
    send(visual.at[theirs], xs.at[roll], v_sem.at[0], v_sem.at[1], partner)
    kv_pass(2)
    far_pass()
    xs[roll] = visual[mine, :]
    text(0, 2)
    for group in range(3):
        kv_end(group)
    far_end()
    def weigh(r):
        start = pl.multiple_of(r * 4096 + z * COLS, COLS)
        xg[r] = (xs[r].astype(F32) * gain_ref[:, pl.ds(start, COLS)]).astype(BF16)

    def half_product(j, r):
        rows = pl.ds(pl.multiple_of(r * COLS, COLS), COLS)
        return jnp.dot(xg[r], kvbuf[j, rows], preferred_element_type=F32)

    weigh(roll)
    own_part[0] = half_product(7, roll)
    own_part[1] = half_product(6 - core, roll)
    arrived(xs.at[1 - roll], v_sem.at[1])
    weigh(1 - roll)

    def product(j):
        return jnp.dot(xg[0], kvbuf[j, :COLS], preferred_element_type=F32) + jnp.dot(
            xg[1], kvbuf[j, COLS:], preferred_element_type=F32
        )

    def sumsq_copy(j):
        sign = 2 * lax.rem(j, 2) - 1
        back = j + sign * (1 - j // 7)
        return pltpu.make_async_remote_copy(
            src_ref=sumsq,
            dst_ref=sumsq_in.at[back],
            send_sem=q_send.at[j],
            recv_sem=q_recv.at[back],
            device_id=at(dz=(j + 1) // 2 * sign),
            device_id_type=MESH,
        )

    def sumsq_send(i, carry):
        sumsq_copy(i).start()
        return carry

    way = 1 - 2 * core

    def ahead(k):
        return 2 * k - 1 + core

    def behind(k):
        return 2 * k - core

    def partial_send(j, dst, slot, steps):
        send(sbuf.at[j], dst.at[slot], p_send.at[j], p_recv.at[slot], at(dz=way * steps))

    total = jnp.zeros((HALF, 1), F32)
    for r in range(2):
        v = xs[r].astype(F32)
        total += jnp.sum(v * v, axis=1, keepdims=True)
    sumsq[...] = jnp.broadcast_to(total, (HALF, HALF)).T[:8]
    lax.fori_loop(1, 8, sumsq_send, 0)
    proj[...] = product(ahead(3))
    sbuf[7] = (own_part[0] + half_product(7, 1 - roll)).astype(BF16)
    partial_send(7, rbuf, 7, 1)
    sbuf[behind(3)] = (own_part[1] + half_product(behind(3), 1 - roll)).astype(BF16)
    partial_send(behind(3), rbuf, 0, -1)
    sbuf[ahead(2)] = product(ahead(2)).astype(BF16)
    partial_send(ahead(2), rbuf, behind(2), 2)
    sbuf[ahead(1)] = product(ahead(1)).astype(BF16)
    partial_send(ahead(1), rbuf, behind(1), 1)
    sbuf[behind(1)] = product(behind(1)).astype(BF16)
    partial_send(behind(1), rbuf, ahead(1), -1)
    arrived(rbuf.at[7], p_recv.at[7])
    sbuf[ahead(3)] = (proj[...] + rbuf[7].astype(F32)).astype(BF16)
    partial_send(ahead(3), rbuf, behind(3), 3)
    proj[...] = product(behind(2))
    arrived(rbuf.at[0], p_recv.at[0])
    sbuf[behind(2)] = (proj[...] + rbuf[0].astype(F32)).astype(BF16)
    partial_send(behind(2), rbuf, ahead(2), -2)
    proj[...] = product(0)
    text(2, 4)
    for copy in started:
        copy.wait_send()
    started.clear()

    def square_step(j, square):
        arrived(sumsq_in.at[j], q_recv.at[j])
        return square + sumsq_in[j]

    square = lax.fori_loop(1, 8, square_step, sumsq[...])
    inv = lax.rsqrt(square * (1.0 / 8192.0) + 1e-06)
    inv = jnp.broadcast_to(inv[:1], (HALF, HALF)).T
    for slot in (ahead(1), behind(1), behind(2), ahead(2), behind(3)):
        arrived(rbuf.at[slot], p_recv.at[slot])
        proj[...] += rbuf[slot].astype(F32)
    key = proj[:, :HEAD_DIM] * inv + kvbias_ref[:, :HEAD_DIM]
    value = proj[:, HEAD_DIM:] * inv + kvbias_ref[:, HEAD_DIM:]
    key = key * cos_ref[...] + pltpu.roll(key, HEAD_DIM // 2, 1) * sin_ref[...]
    res[:, :HEAD_DIM] = key.astype(BF16)
    res[:, HEAD_DIM:] = value.astype(BF16)
    send(res, res_in, o_sem.at[0], o_sem.at[1], partner)
    out_ref[mine, :] = res[...]
    text(6, 2)
    arrived(res_in, o_sem.at[1])
    out_ref[theirs, :] = res_in[...]
    for copy in started:
        copy.wait_send()

    def sent_step(j, carry):
        sumsq_copy(j).wait_send()
        return carry

    lax.fori_loop(1, 8, sent_step, 0)


def gather_project(vis, w, kvw, mbias, gain, kvbias, pos, q, tkv):
    rollouts = q.shape[0] // RLEN
    heads = q.shape[1] // HEAD_DIM
    vmem = pl.BlockSpec(memory_space=pltpu.VMEM)
    hbm = pl.BlockSpec(memory_space=pltpu.HBM)
    dma = pltpu.SemaphoreType.DMA
    return pl.pallas_call(
        gather_project_kernel,
        out_shape=(
            pltpu.VMEM((ROWS, 2 * HEAD_DIM), BF16),
            pltpu.VMEM((rollouts, heads * RLEN, 2 * HEAD_DIM), F32),
            pltpu.VMEM((rollouts, heads * RLEN, HEAD_DIM), F32),
        ),
        in_specs=[hbm] * 9,
        out_specs=(vmem, vmem, vmem),
        scratch_shapes=[
            pltpu.VMEM((1, COLS), F32),
            pltpu.VMEM((1, 8192), F32),
            pltpu.VMEM((1, 2 * HEAD_DIM), F32),
            pltpu.VMEM((3, ROWS), jnp.int32),
            pltpu.VMEM((HALF, HEAD_DIM), F32),
            pltpu.VMEM((HALF, HEAD_DIM), F32),
            pltpu.VMEM(q.shape, BF16),
            pltpu.VMEM(tkv.shape, BF16),
            pltpu.VMEM((ROWS, 5120), BF16),
            pltpu.VMEM((8, ROWS, PAIR), BF16),
            pltpu.VMEM((8, PAIR, COLS), BF16),
            pltpu.VMEM((8, 1024, 2 * HEAD_DIM), BF16),
            pltpu.VMEM((ROWS, COLS), F32),
            pltpu.VMEM((ROWS, COLS), BF16),
            pltpu.VMEM((2, HALF, COLS), BF16),
            pltpu.VMEM((2, HALF, COLS), BF16),
            pltpu.VMEM((8, HALF), F32),
            pltpu.VMEM((8, 8, HALF), F32),
            pltpu.VMEM((8, HALF, 2 * HEAD_DIM), BF16),
            pltpu.VMEM((8, HALF, 2 * HEAD_DIM), BF16),
            pltpu.VMEM((HALF, 2 * HEAD_DIM), F32),
            pltpu.VMEM((2, HALF, 2 * HEAD_DIM), F32),
            pltpu.VMEM((HALF, 2 * HEAD_DIM), BF16),
            pltpu.VMEM((HALF, 2 * HEAD_DIM), BF16),
            dma((9,)),
            dma((32,)),
            dma((32,)),
            dma((8,)),
            dma((8,)),
            dma((19,)),
            dma((19,)),
            dma((2,)),
            dma((8,)),
            dma((8,)),
            dma((8,)),
            dma((8,)),
            dma((2,)),
        ],
        compiler_params=pltpu.CompilerParams(
            collective_id=0, has_side_effects=True, vmem_limit_bytes=46 * 2**20
        ),
        cost_estimate=pl.CostEstimate(
            flops=2_500_000_000, bytes_accessed=8_000_000, transcendentals=1_500_000
        ),
        name="gather_project",
    )(vis, w, kvw, mbias, gain, kvbias, pos, q, tkv)


def attention_kernel(
    count_ref,
    length_ref,
    q_in,
    kv_in,
    text_sums,
    text_max,
    out_hbm,
    out,
    keys,
    values,
    out_sem,
):
    rollouts = length_ref.shape[0]
    live = lax.broadcasted_iota(jnp.int32, (ROWS, HEAD_DIM), 0) < count_ref[0]
    image_keys = kv_in[:, :HEAD_DIM]
    keys[...] = jnp.where(live, image_keys, image_keys[:1])
    values[:, :HEAD_DIM] = jnp.where(live, kv_in[:, HEAD_DIM:], 0.0).astype(BF16)
    values[:, HEAD_DIM:] = jnp.where(live, 1.0, 0.0).astype(BF16)
    token = lax.rem(lax.broadcasted_iota(jnp.int32, (8 * RLEN, RLEN), 0), RLEN)
    heads = [slice(h * HEAD_DIM, (h + 1) * HEAD_DIM) for h in range(8)]

    def one(r):
        rows = pl.ds(pl.multiple_of(r * RLEN, RLEN), RLEN)
        kept = token < length_ref[r]
        q = jnp.concatenate([q_in[rows, cols] for cols in heads], axis=0)
        scores = lax.dot_general(
            q, keys[...], (((1,), (1,)), ((), ())), preferred_element_type=F32
        )
        first, second = scores[:, :HEAD_DIM], scores[:, HEAD_DIM:]
        text_highest = text_max[r]
        highest = jnp.max(jnp.maximum(first, second), axis=1, keepdims=True)
        highest = jnp.maximum(highest, text_highest)
        first = jnp.exp2((first - highest) * SCORE_FACTOR)
        second = jnp.exp2((second - highest) * SCORE_FACTOR)
        scale = jnp.exp2((text_highest - highest) * SCORE_FACTOR)
        weights = jnp.concatenate([first, second], axis=1).astype(BF16)
        sums = jnp.dot(weights, values[...], preferred_element_type=F32)
        top = sums[:, :HEAD_DIM] + text_sums[r, :, :HEAD_DIM] * scale
        bottom = sums[:, HEAD_DIM:] + text_sums[r, :, HEAD_DIM:] * scale
        attended = jnp.where(kept, top / bottom, 0.0).astype(BF16)
        for i, cols in enumerate(heads):
            out[r, :, cols] = attended[i * RLEN : (i + 1) * RLEN]

    def store(r):
        rows = pl.ds(pl.multiple_of(r * RLEN, RLEN), RLEN)
        return pltpu.make_async_copy(out.at[r], out_hbm.at[rows], out_sem.at[r])

    def step(i, carry):
        for u in range(UNROLL):
            one(i * UNROLL + u)
            store(i * UNROLL + u).start()
        return carry

    lax.fori_loop(0, rollouts // UNROLL, step, 0)

    def stored(r, carry):
        store(r).wait()
        return carry

    lax.fori_loop(0, rollouts, stored, 0)


def attention(count, length, q, kv, text_sums, text_max):
    rollouts = length.shape[0]
    smem = pl.BlockSpec(memory_space=pltpu.SMEM)
    vmem = pl.BlockSpec(memory_space=pltpu.VMEM)
    return pl.pallas_call(
        attention_kernel,
        in_specs=[smem, smem, vmem, vmem, vmem, vmem],
        out_specs=pl.BlockSpec(memory_space=pl.ANY),
        out_shape=jax.ShapeDtypeStruct(q.shape, BF16),
        scratch_shapes=[
            pltpu.VMEM((rollouts, RLEN, q.shape[1]), BF16),
            pltpu.VMEM((ROWS, HEAD_DIM), BF16),
            pltpu.VMEM((ROWS, 2 * HEAD_DIM), BF16),
            pltpu.SemaphoreType.DMA((rollouts,)),
        ],
        compiler_params=pltpu.CompilerParams(vmem_limit_bytes=24 * 2**20),
        name="attention",
    )(count, length, q, kv, text_sums, text_max)


def body(
    vis_hidden,
    merge_weight,
    merge_bias,
    norm_gain,
    kv_weight,
    kv_bias,
    queries,
    text_kv,
    image_count,
    image_pos,
    resp_length,
):
    kv, text_sums, text_max = gather_project(
        vis_hidden,
        merge_weight,
        kv_weight,
        merge_bias.reshape(1, -1),
        norm_gain.reshape(1, -1),
        kv_bias.reshape(1, -1),
        image_pos,
        queries,
        text_kv,
    )
    return attention(image_count, resp_length, queries, kv, text_sums, text_max)


def solution(mesh):
    in_specs = (
        P("group", None),
        P("group", ("roll", "tp")),
        P(("roll", "tp")),
        P(),
        P(None, "tp"),
        P("tp"),
        P(("group", "roll"), "tp"),
        P(("group", "roll"), "tp"),
        P("group"),
        P(None, "group"),
        P(("group", "roll")),
    )
    out_specs = P(("group", "roll"), "tp")
    return jax.shard_map(body, mesh=mesh, in_specs=in_specs, out_specs=out_specs, check_vma=False)
```
